512 devices in a mesh: dp: 32 (over y, z_lo, core), shard: 16 (over x, z_hi).
Axes of the slice: x: 4, y: 8, z: 8 (z_hi: 4, z_lo: 2; z = z_hi * 2 + z_lo), core: 2. Of those that a mesh axis runs over, the one named last changes fastest.
Arguments:
- queries: bfloat16 [65536, 2048], P(('dp', 'shard')), may hold values from -6 to 6
- keys_in: bfloat16 [65536, 2048], P(('dp', 'shard')), may hold values from -6 to 6
- values: bfloat16 [65536, 2048], P(('dp', 'shard')), may hold values from -6 to 6
- out_grad: bfloat16 [65536, 2048], P(('dp', 'shard')), may hold values from -48 to 48
- out_weight: bfloat16 [2048, 2048], P('shard'), may hold values from -0.125 to 0.125
- block_lists: int32 [32, 16, 4], P('dp'), may hold values from 0 to 15, as said below
- voxel_count: int32 [32], P('dp'), may hold values from 1024 to 2048
Outputs:
- grad_query: bfloat16 [65536, 2048], P(('dp', 'shard'))
- grad_key: bfloat16 [65536, 2048], P(('dp', 'shard'))
- grad_value: bfloat16 [65536, 2048], P(('dp', 'shard'))
- grad_weight: bfloat16 [2048, 2048], P('shard')
The draws below stay inside these ranges and needn't reach their ends.
Inputs may be any that keep to these rules, and one draw needn't show every extreme that they name: `block_lists`: entry 0 of row b of a scene's list is b itself; the 4 entries of a row are different blocks of that scene.
All inputs are finite; a program needn't handle non-finite values.
Results may differ from the reference program's by a relative error of at most 0.0095.
Values may be sent and summed in bfloat16 or wider, within the bound.
A program may use at most 128 MiB of HBM per device.

```python
import math
import jax
import jax.numpy as jnp
from jax import lax

HEADS = 16
HDIM = 128
OUTW = 2048
BLOCK = 128
NB = 4
SCENE_TOK = 2048
NBLK = 16
SCENES = 32
TOKENS = 65536


def draw_queries(key, part):
    key = jax.random.fold_in(key, 11)
    return jnp.clip(jax.random.normal(key, (TOKENS, HEADS * HDIM)), -4.0, 4.0).astype(jnp.bfloat16)


def draw_keys_in(key, part):
    key = jax.random.fold_in(key, 13)
    return jnp.clip(jax.random.normal(key, (TOKENS, HEADS * HDIM)), -4.0, 4.0).astype(jnp.bfloat16)


def draw_block_lists(key, part):
    key = jax.random.fold_in(key, 17)
    picks = jax.random.randint(key, (SCENES, NBLK, NBLK - 1), 0, 2 ** 20) * NBLK + jnp.arange(NBLK - 1, dtype=jnp.int32)
    unused, offsets = lax.top_k(picks, NB - 1)
    own_block = jnp.broadcast_to(jnp.arange(NBLK, dtype=jnp.int32)[None, :, None], (SCENES, NBLK, 1))
    others = (own_block + offsets.astype(jnp.int32) + 1) % NBLK
    return jnp.concatenate([own_block, others], axis=-1).astype(jnp.int32)


def touch_ends(entries, rng, smallest, high):
    index_at = [jax.random.randint(jax.random.fold_in(rng, axis), (), 0, length) for axis, length in enumerate(entries.shape)]
    main_axis = entries.shape.index(max(entries.shape))
    beside = index_at[:main_axis] + [(index_at[main_axis] + 1) % entries.shape[main_axis]] + index_at[main_axis + 1:]
    return entries.at[tuple(index_at)].set(smallest).at[tuple(beside)].set(high)


def block_scale(key, dims, shards, low, high):
    gain = 1.0
    for dim, parts in shards:
        draws = jax.random.uniform(jax.random.fold_in(jax.random.fold_in(key, 6), dim), (parts,), jnp.float32, low / len(shards), high / len(shards))
        gain = gain * jnp.repeat(jnp.exp(draws), dims[dim] // parts).reshape((-1,) + (1,) * (len(dims) - 1 - dim))
    return gain


def scatter_about(stream_key, shape, deviation, limit, cuts=(), kind=jnp.bfloat16):
    level = block_scale(stream_key, shape, cuts, -0.22, 0.18) if cuts else 1.0
    entries = jax.random.normal(stream_key, shape, jnp.float32) * deviation * level
    return jnp.minimum(jnp.maximum(entries, -limit), limit).astype(kind)


def setup_inputs(seed: int = 0) -> dict:
    streams_of = jax.random.split(jax.random.key(seed), 8)
    return {
        "queries": draw_queries(jax.random.fold_in(streams_of[7], 71), 0),
        "keys_in": draw_keys_in(jax.random.fold_in(streams_of[7], 71), 0),
        "values": scatter_about(streams_of[2], (TOKENS, HEADS * HDIM), 1.0, 6.0, ((0, 512),)),
        "out_grad": scatter_about(streams_of[3], (TOKENS, OUTW), 8.0, 48.0, ((0, 512),)),
        "out_weight": scatter_about(streams_of[4], (HEADS * HDIM, OUTW), (HEADS * HDIM) ** -0.5, 0.125, ((0, 16),)),
        "block_lists": draw_block_lists(jax.random.fold_in(streams_of[7], 71), 0),
        "voxel_count": touch_ends(jax.random.randint(streams_of[6], (SCENES,), SCENE_TOK // 2, SCENE_TOK + 1), jax.random.fold_in(streams_of[6], 1), SCENE_TOK // 2, SCENE_TOK).astype(jnp.int32),
    }


def attend(queries, keys_in, values, block_ids, live_count):
    row_count, width_all = queries.shape
    head_count = width_all // HDIM
    block_count = row_count // BLOCK
    score_scale = 1.0 / math.sqrt(HDIM)
    query_blk = queries.reshape(block_count, BLOCK, head_count, HDIM).astype(jnp.float32)
    key_blk = keys_in.reshape(block_count, BLOCK, head_count, HDIM)[block_ids].reshape(block_count, NB * BLOCK, head_count, HDIM).astype(jnp.float32)
    value_blk = values.reshape(block_count, BLOCK, head_count, HDIM)[block_ids].reshape(block_count, NB * BLOCK, head_count, HDIM).astype(jnp.float32)
    query_pos = jnp.arange(row_count, dtype=jnp.int32).reshape(block_count, BLOCK)
    key_pos = (block_ids[:, :, None] * BLOCK + jnp.arange(BLOCK, dtype=jnp.int32)[None, None, :]).reshape(block_count, NB * BLOCK)
    allowed = (key_pos[:, None, :] < live_count) | (query_pos[:, :, None] >= live_count)
    scores = jnp.einsum('bqhd,bkhd->bhqk', query_blk, key_blk) * score_scale
    scores = jnp.where(allowed[:, None], scores, -jnp.inf)
    peak = lax.optimization_barrier(jnp.max(scores, axis=-1, keepdims=True))
    weights = jnp.exp(scores - peak)
    probs = weights / lax.optimization_barrier(jnp.sum(weights, axis=-1, keepdims=True))
    return (query_blk, key_blk, value_blk, probs)

def scene_pass(queries, keys_in, values, grad_out, out_weight, block_ids, live_count):
    row_count, width_all = queries.shape
    head_count = width_all // HDIM
    block_count = row_count // BLOCK
    score_scale = 1.0 / math.sqrt(HDIM)
    is_live = jnp.arange(row_count, dtype=jnp.int32) < live_count
    grad_live = jnp.where(is_live[:, None], grad_out, jnp.zeros_like(grad_out))
    query_blk, key_blk, value_blk, probs = attend(queries, keys_in, values, block_ids, live_count)
    prob_bf = lax.optimization_barrier(probs.astype(jnp.bfloat16)).astype(jnp.float32)
    heads_out = jnp.einsum('bhqk,bkhd->bqhd', prob_bf, value_blk).reshape(row_count, width_all).astype(jnp.bfloat16)
    grad_attn = jnp.dot(grad_live, out_weight.T, preferred_element_type=jnp.float32).astype(jnp.bfloat16)
    weight_sum = jnp.dot(heads_out.T, grad_live, preferred_element_type=jnp.float32)
    grad_o = lax.optimization_barrier(grad_attn).reshape(block_count, BLOCK, head_count, HDIM).astype(jnp.float32)
    grad_prob = jnp.einsum('bqhd,bkhd->bhqk', grad_o, value_blk)
    row_delta = lax.optimization_barrier(jnp.sum(probs * grad_prob, axis=-1, keepdims=True))
    dscore = (probs * (grad_prob - row_delta) * score_scale).astype(jnp.bfloat16)
    dscore = lax.optimization_barrier(dscore).astype(jnp.float32)
    grad_query = jnp.einsum('bhqk,bkhd->bqhd', dscore, key_blk).reshape(row_count, width_all).astype(jnp.bfloat16)
    onehot = (block_ids[:, :, None] == jnp.arange(block_count, dtype=jnp.int32)[None, None, :]).astype(jnp.float32)
    key_parts = jnp.einsum('bhqk,bqhd->bkhd', dscore, query_blk).reshape(block_count, NB, BLOCK, width_all)
    value_parts = jnp.einsum('bhqk,bqhd->bkhd', prob_bf, grad_o).reshape(block_count, NB, BLOCK, width_all)
    grad_key = jnp.einsum('bjc,bjrx->crx', onehot, key_parts, precision=lax.Precision.HIGHEST).reshape(row_count, width_all).astype(jnp.bfloat16)
    grad_value = jnp.einsum('bjc,bjrx->crx', onehot, value_parts, precision=lax.Precision.HIGHEST).reshape(row_count, width_all).astype(jnp.bfloat16)
    return (grad_query, grad_key, grad_value, weight_sum)

def reference(queries, keys_in, values, out_grad, out_weight, block_lists, voxel_count):
    scene_shape = (SCENES, SCENE_TOK, -1)
    stacked = (queries.reshape(scene_shape), keys_in.reshape(scene_shape), values.reshape(scene_shape), out_grad.reshape(scene_shape), block_lists, voxel_count)

    def scene_step(running, scene_item):
        query_s, key_s, value_s, grad_s, ids_s, count_s = scene_item
        grad_query, grad_key, grad_value, weight_sum = scene_pass(query_s, key_s, value_s, grad_s, out_weight, ids_s, count_s)
        return (running + weight_sum, (grad_query, grad_key, grad_value))
    start_sum = jnp.zeros((HEADS * HDIM, OUTW), jnp.float32)
    running, (grad_query, grad_key, grad_value) = lax.scan(scene_step, start_sum, stacked)
    flat_shape = (TOKENS, HEADS * HDIM)
    grad_weight = (running / SCENES).astype(jnp.bfloat16)
    return (grad_query.reshape(flat_shape), grad_key.reshape(flat_shape), grad_value.reshape(flat_shape), grad_weight)
```

```python
import math

import jax
import jax.numpy as jnp
from jax import lax
from jax.experimental import pallas as pl
from jax.experimental.pallas import tpu as pltpu
from jax.sharding import PartitionSpec as P

HDIM = 128
BLOCK = 128
NB = 4
NBLK = 16
WIDTH = 2048
HALF = BLOCK // 2
SCALE = 1.0 / math.sqrt(HDIM)
LOG2E = math.log2(math.e)
F32 = jnp.float32
BF16 = jnp.bfloat16
MESH = pl.DeviceIdType.MESH

NT = (((1,), (1,)), ((), ()))
NN = (((1,), (0,)), ((), ()))


def dot(a, b, dims):
    return lax.dot_general(a, b, dims, preferred_element_type=F32)


def order(i):
    return i + i // 2 - 2 * (i // 3)


def kernel(
    parts,
    q_in, k_in, v_in, g_in, w_ref, lists, count,
    dq_out, dk_out, dv_out, dw_out,
    qh, kh, vh, kt, vt, gall, probs, heads, dqb, kpart, vpart, kacc, vacc, dkb, dvb,
    wacc, wbf, wrecv, wres,
    qkv_recv, g_recv, out_recv, w_recv, send_sem, local_sem,
):
    me = lax.axis_index("shard")
    scene = lax.axis_index("dp")
    row_parts, col_parts = parts
    scenes = row_parts * col_parts
    wrow, wcol = BLOCK // row_parts, WIDTH // col_parts
    x, z = me // 4, me % 4
    x_up, x_down = ((x + 1) % 4) * 4 + z, ((x + 3) % 4) * 4 + z
    z_up, z_down = x * 4 + (z + 1) % 4, x * 4 + (z + 3) % 4
    live = count[0]

    def columns(index):
        return pl.ds(pl.multiple_of(index * HDIM, HDIM), HDIM)

    barrier = pltpu.get_barrier_semaphore()

    @pl.loop(1, NBLK)
    def _(o):
        pl.semaphore_signal(barrier, inc=1, device_id={"shard": (me + o) % NBLK}, device_id_type=MESH)

    @pl.loop(1, scenes)
    def _(o):
        pl.semaphore_signal(barrier, inc=1, device_id={"dp": (scene + o) % scenes}, device_id_type=MESH)

    pl.semaphore_wait(barrier, NBLK - 1 + scenes - 1)

    def push(src, dst, send, recv, shard):
        pltpu.make_async_remote_copy(
            src_ref=src, dst_ref=dst, send_sem=send, recv_sem=recv,
            device_id={"shard": shard}, device_id_type=MESH,
        ).start()

    def await_bytes(ref, sem):
        pltpu.make_async_copy(ref, ref, sem).wait()

    def block_at(dx, dz):
        return ((x + dx) % 4) * 4 + (z + dz) % 4

    def g_ref(dx, dz, half):
        ref = gall.at[block_at(dx, dz)]
        return ref if half is None else ref.at[pl.ds(half * HALF, HALF)]

    def g_push(src, dx, dz, half, target, rdx, rdz):
        push(src, g_ref(dx, dz, half), send_sem.at[0],
             g_recv.at[rdx * 4 + rdz, 0 if half is None else half], target)

    def g_wait(dx, dz, half):
        await_bytes(g_ref(dx, dz, half), g_recv.at[dx * 4 + dz, 0 if half is None else half])

    def g_along_x(src, dz, half):
        g_push(src, 0, dz, half, x_up, 3, dz)
        g_push(src, 0, dz, half, x_down, 1, dz)

    g_push(g_in, 0, 0, None, z_up, 0, 3)
    g_push(g_in, 0, 0, None, z_down, 0, 1)
    g_along_x(g_in, 0, None)
    for i, (src, dst) in enumerate(((q_in, qh), (k_in, kh), (v_in, vh))):
        @pl.loop(1, NBLK)
        def _(o, i=i, src=src, dst=dst):
            peer = (me + o) % NBLK
            push(src.at[:, columns(peer)], dst.at[me], send_sem.at[1], qkv_recv.at[i], peer)

    own = [
        pltpu.make_async_copy(g_in, gall.at[me], local_sem.at[0]),
        pltpu.make_async_copy(q_in.at[:, columns(me)], qh.at[me], local_sem.at[1]),
        pltpu.make_async_copy(k_in.at[:, columns(me)], kh.at[me], local_sem.at[2]),
        pltpu.make_async_copy(v_in.at[:, columns(me)], vh.at[me], local_sem.at[3]),
    ]
    for copy in own:
        copy.start()
    kacc[...] = jnp.zeros_like(kacc)
    vacc[...] = jnp.zeros_like(vacc)
    for copy in own:
        copy.wait()

    def forward_x(dz, first, second):
        g_wait(3, dz, first)
        g_push(g_ref(3, dz, 0), 3, dz, 0, x_up, 2, dz)
        g_wait(1, dz, second)
        g_push(g_ref(1, dz, 1), 1, dz, 1, x_down, 2, dz)

    forward_x(0, None, None)
    g_wait(0, 3, None)
    g_push(g_ref(0, 3, 0), 0, 3, 0, z_up, 0, 2)
    g_along_x(g_ref(0, 3, None), 3, None)
    g_wait(0, 1, None)
    g_push(g_ref(0, 1, 1), 0, 1, 1, z_down, 0, 2)
    g_along_x(g_ref(0, 1, None), 1, None)
    for half in range(2):
        g_wait(0, 2, half)
        g_along_x(g_ref(0, 2, half), 2, half)
    forward_x(3, None, None)
    forward_x(1, None, None)

    for i, dst in enumerate((qh, kh, vh)):
        await_bytes(dst.at[pl.ds(0, NBLK - 1)], qkv_recv.at[i])

    @pl.loop(0, NBLK)
    def _(b):
        kt[b] = kh[b].T
        vt[b] = vh[b].T

    lane = lax.broadcasted_iota(jnp.int32, (BLOCK, BLOCK), 1)
    sublane = lax.broadcasted_iota(jnp.int32, (BLOCK, BLOCK), 0)

    @pl.loop(0, NBLK)
    def _(b):
        ids = [lists[0, b, j] for j in range(NB)]
        keys = jnp.concatenate([kh[c] for c in ids], axis=0)
        scores = dot(keys, qh[b], NT) * (SCALE * LOG2E)
        query_pos = b * BLOCK + lane
        dead_query = query_pos >= live
        allowed = jnp.concatenate([((c * BLOCK + sublane) < live) | dead_query for c in ids], axis=0)
        scores = jnp.where(allowed, scores, -jnp.inf)
        peak = jnp.max(scores, axis=0, keepdims=True)
        weights = jnp.exp2(scores - peak)
        prob = weights * (1.0 / jnp.sum(weights, axis=0, keepdims=True))
        probs[b] = prob
        values_t = jnp.concatenate([vt[c] for c in ids], axis=1)
        head_t = dot(values_t, prob.astype(BF16), NN)
        heads[:, columns(b)] = jnp.where(dead_query, 0.0, head_t).astype(BF16)

    forward_x(2, 0, 1)
    g_wait(3, 2, 1)
    g_wait(1, 2, 0)

    def backward(b):
        ids = [lists[0, b, j] for j in range(NB)]
        dead_query = (b * BLOCK + lane) >= live
        da_t = jnp.where(dead_query, 0.0, dot(w_ref[...], gall[b], NT)).astype(BF16)
        prob = probs[b]
        grad_prob = dot(jnp.concatenate([vh[c] for c in ids], axis=0), da_t, NN)
        delta = jnp.sum(prob * grad_prob, axis=0, keepdims=True)
        dscore = (prob * (grad_prob - delta) * SCALE).astype(BF16)
        keys_t = jnp.concatenate([kt[c] for c in ids], axis=1)
        dqb[b] = dot(keys_t, dscore, NN).T.astype(BF16)
        kpart[...] = dot(dscore, qh[b], NN).reshape(NB, BLOCK, HDIM)
        vpart[...] = dot(prob.astype(BF16), da_t, NT).reshape(NB, BLOCK, HDIM)
        for c in range(NBLK):
            place, gain = 0, 0.0
            for j in range(NB):
                place = jnp.where(ids[j] == c, j, place)
                gain = jnp.where(ids[j] == c, 1.0, gain)
            kacc[c] += gain * kpart[place]
            vacc[c] += gain * vpart[place]

    def send_dq(b):
        push(dqb.at[b], dq_out.at[:, columns(me)], send_sem.at[1], out_recv.at[0], b)

    @pl.loop(0, 12)
    def _(t):
        b = block_at(order(t % 3), order(t // 3))
        backward(b)

        @pl.when(t > 0)
        def _():
            send_dq(b)

    @pl.loop(0, 4)
    def _(t):
        dz = order(t)
        b = block_at(2, dz)
        await_bytes(gall.at[b, pl.ds(0, HALF)], g_recv.at[8 + dz, 0])
        await_bytes(gall.at[b, pl.ds(HALF, HALF)], g_recv.at[8 + dz, 1])
        backward(b)
        send_dq(b)

    dkb[...] = kacc[...].astype(BF16)
    dvb[...] = vacc[...].astype(BF16)

    @pl.loop(1, NBLK)
    def _(o):
        peer = (me + o) % NBLK
        push(dkb.at[peer], dk_out.at[:, columns(me)], send_sem.at[1], out_recv.at[1], peer)
        push(dvb.at[peer], dv_out.at[:, columns(me)], send_sem.at[1], out_recv.at[2], peer)

    back = [
        pltpu.make_async_copy(src.at[me], dst.at[:, columns(me)], local_sem.at[i])
        for i, (src, dst) in enumerate(((dqb, dq_out), (dkb, dk_out), (dvb, dv_out)))
    ]
    for copy in back:
        copy.start()

    tile = 256

    @pl.loop(0, WIDTH // tile)
    def _(t):
        at = pl.ds(pl.multiple_of(t * tile, tile), tile)
        out = dot(heads[...], gall[:, :, at].reshape(NBLK * BLOCK, tile), NN)
        wacc[:, at] = out
        wbf[:, at] = out.astype(BF16)

    def piece(index):
        return (
            pl.ds(pl.multiple_of((index // col_parts) * wrow, wrow), wrow),
            pl.ds(pl.multiple_of((index % col_parts) * wcol, wcol), wcol),
        )

    def push_dp(src, dst, send, recv, peer):
        pltpu.make_async_remote_copy(
            src_ref=src, dst_ref=dst, send_sem=send, recv_sem=recv,
            device_id={"dp": peer}, device_id_type=MESH,
        ).start()

    @pl.loop(1, scenes)
    def _(o):
        peer = (scene + o) % scenes
        push_dp(wbf.at[piece(peer)], wrecv.at[o - 1], send_sem.at[2], w_recv.at[0], peer)

    await_bytes(wrecv, w_recv.at[0])
    total = wacc[piece(scene)]
    for i in range(scenes - 1):
        total = total + wrecv[i].astype(F32)
    wres[...] = (total * (1.0 / scenes)).astype(BF16)

    @pl.loop(1, scenes)
    def _(o):
        peer = (scene + o) % scenes
        push_dp(wres, dw_out.at[piece(scene)], send_sem.at[3], w_recv.at[1], peer)

    keep = pltpu.make_async_copy(wres, dw_out.at[piece(scene)], local_sem.at[3])
    keep.start()
    keep.wait()
    for copy in back:
        copy.wait()
    await_bytes(wrecv, w_recv.at[1])
    for i, out in enumerate((dq_out, dk_out, dv_out)):
        await_bytes(out.at[:, pl.ds(0, WIDTH - HDIM)], out_recv.at[i])
    await_bytes(gall.at[pl.ds(0, NBLK - 1)], send_sem.at[0])
    for dst in (qh, kh, vh, dqb, dkb, dvb):
        await_bytes(dst.at[pl.ds(0, NBLK - 1)], send_sem.at[1])
    await_bytes(wrecv, send_sem.at[2])
    await_bytes(wrecv, send_sem.at[3])


def body(queries, keys_in, values, out_grad, out_weight, block_lists, voxel_count):
    scenes = lax.axis_size("dp")
    row_parts = min(8, scenes)
    col_parts = scenes // row_parts
    wrow, wcol = BLOCK // row_parts, WIDTH // col_parts
    blocks = (NBLK, BLOCK, HDIM)
    hbm = pl.BlockSpec(memory_space=pl.ANY)
    vmem = pl.BlockSpec(memory_space=pltpu.VMEM)
    smem = pl.BlockSpec(memory_space=pltpu.SMEM)
    rows = jax.ShapeDtypeStruct((BLOCK, WIDTH), BF16)

    def run(*refs):
        kernel((row_parts, col_parts), *refs)

    return pl.pallas_call(
        run,
        out_shape=(rows, rows, rows, rows),
        in_specs=[hbm, hbm, hbm, hbm, vmem, smem, smem],
        out_specs=(hbm, hbm, hbm, hbm),
        scratch_shapes=[
            pltpu.VMEM(blocks, BF16),
            pltpu.VMEM(blocks, BF16),
            pltpu.VMEM(blocks, BF16),
            pltpu.VMEM(blocks, BF16),
            pltpu.VMEM(blocks, BF16),
            pltpu.VMEM((NBLK, BLOCK, WIDTH), BF16),
            pltpu.VMEM((NBLK, NB * BLOCK, BLOCK), F32),
            pltpu.VMEM((HDIM, NBLK * BLOCK), BF16),
            pltpu.VMEM(blocks, BF16),
            pltpu.VMEM((NB, BLOCK, HDIM), F32),
            pltpu.VMEM((NB, BLOCK, HDIM), F32),
            pltpu.VMEM(blocks, F32),
            pltpu.VMEM(blocks, F32),
            pltpu.VMEM(blocks, BF16),
            pltpu.VMEM(blocks, BF16),
            pltpu.VMEM((BLOCK, WIDTH), F32),
            pltpu.VMEM((BLOCK, WIDTH), BF16),
            pltpu.VMEM((scenes - 1, wrow, wcol), BF16),
            pltpu.VMEM((wrow, wcol), BF16),
            pltpu.SemaphoreType.DMA((3,)),
            pltpu.SemaphoreType.DMA((16, 2)),
            pltpu.SemaphoreType.DMA((3,)),
            pltpu.SemaphoreType.DMA((2,)),
            pltpu.SemaphoreType.DMA((4,)),
            pltpu.SemaphoreType.DMA((4,)),
        ],
        compiler_params=pltpu.CompilerParams(
            collective_id=0, has_side_effects=True, vmem_limit_bytes=48 * 1024 * 1024
        ),
        cost_estimate=pl.CostEstimate(flops=4_000_000_000, bytes_accessed=8_000_000, transcendentals=1_000_000),
    )(queries, keys_in, values, out_grad, out_weight, block_lists, voxel_count)


def solution(mesh):
    return jax.shard_map(
        body,
        mesh=mesh,
        in_specs=(
            P(("dp", "shard"), None),
            P(("dp", "shard"), None),
            P(("dp", "shard"), None),
            P(("dp", "shard"), None),
            P("shard", None),
            P("dp", None, None),
            P("dp"),
        ),
        out_specs=(
            P(("dp", "shard"), None),
            P(("dp", "shard"), None),
            P(("dp", "shard"), None),
            P("shard", None),
        ),
        check_vma=False,
    )
```

```python
import math

import jax
import jax.numpy as jnp
from jax import lax
from jax.experimental import pallas as pl
from jax.experimental.pallas import tpu as pltpu
from jax.sharding import PartitionSpec as P

HDIM = 128
BLOCK = 128
NB = 4
NBLK = 16
WIDTH = 2048
HALF = BLOCK // 2
QUART = BLOCK // 4
SCALE = 1.0 / math.sqrt(HDIM)
LOG2E = math.log2(math.e)
F32 = jnp.float32
BF16 = jnp.bfloat16
MESH = pl.DeviceIdType.MESH

NT = (((1,), (1,)), ((), ()))
NN = (((1,), (0,)), ((), ()))


def dot(a, b, dims):
    return lax.dot_general(a, b, dims, preferred_element_type=F32)


def order(i):
    return i + i // 2 - 2 * (i // 3)


def kernel(
    parts,
    q_in, k_in, v_in, g_in, w_in, lists, count,
    dq_out, dk_out, dv_out, dw_out,
    qh, kh, vh, kt, vt, gall, probs, heads, dqb, kpart, vpart, kacc, vacc, dkb, dvb,
    w_ref, wacc, wbf, wcore, whalf, whbf, wquart, wqbf, wrecv, wres,
    qkv_recv, g_recv, out_recv, w_recv, send_sem, local_sem,
):
    me = lax.axis_index("shard")
    scene = lax.axis_index("dp")
    row_parts, col_parts = parts
    rows_y = row_parts * col_parts
    scenes = 4 * rows_y
    wrow, wcol = QUART // row_parts, WIDTH // col_parts
    core, low, y = scene % 2, (scene // 2) % 2, scene // 4
    x, z = me // 4, me % 4
    x_up, x_down = ((x + 1) % 4) * 4 + z, ((x + 3) % 4) * 4 + z
    z_up, z_down = x * 4 + (z + 1) % 4, x * 4 + (z + 3) % 4
    live = count[0]

    def columns(index):
        return pl.ds(pl.multiple_of(index * HDIM, HDIM), HDIM)

    own = [
        pltpu.make_async_copy(g_in, gall.at[me], local_sem.at[0]),
        pltpu.make_async_copy(q_in.at[:, columns(me)], qh.at[me], local_sem.at[1]),
        pltpu.make_async_copy(k_in.at[:, columns(me)], kh.at[me], local_sem.at[2]),
        pltpu.make_async_copy(v_in.at[:, columns(me)], vh.at[me], local_sem.at[3]),
        pltpu.make_async_copy(w_in, w_ref, local_sem.at[4]),
    ]
    for copy in own:
        copy.start()

    barrier = pltpu.get_barrier_semaphore()

    @pl.loop(1, NBLK)
    def _(o):
        pl.semaphore_signal(barrier, inc=1, device_id={"shard": (me + o) % NBLK}, device_id_type=MESH)

    @pl.loop(1, rows_y)
    def _(o):
        pl.semaphore_signal(
            barrier, inc=1, device_id={"dp": ((y + o) % rows_y) * 4 + scene % 4}, device_id_type=MESH
        )

    other_core = scene + 1 - 2 * core
    other_low = scene + 2 - 4 * low
    for peer in (other_core, other_low):
        pl.semaphore_signal(barrier, inc=1, device_id={"dp": peer}, device_id_type=MESH)
    pl.semaphore_wait(barrier, NBLK - 1 + rows_y - 1 + 2)

    def push(src, dst, send, recv, shard):
        pltpu.make_async_remote_copy(
            src_ref=src, dst_ref=dst, send_sem=send, recv_sem=recv,
            device_id={"shard": shard}, device_id_type=MESH,
        ).start()

    def push_dp(src, dst, send, recv, peer):
        pltpu.make_async_remote_copy(
            src_ref=src, dst_ref=dst, send_sem=send, recv_sem=recv,
            device_id={"dp": peer}, device_id_type=MESH,
        ).start()

    def await_bytes(ref, sem):
        pltpu.make_async_copy(ref, ref, sem).wait()

    def block_at(dx, dz):
        return ((x + dx) % 4) * 4 + (z + dz) % 4

    def g_ref(dx, dz, half):
        return gall.at[block_at(dx, dz), pl.ds(half * HALF, HALF)]

    def g_push(dx, dz, half, target, rdx, rdz):
        src = g_in.at[pl.ds(half * HALF, HALF)] if (dx, dz) == (0, 0) else g_ref(dx, dz, half)
        push(src, g_ref(dx, dz, half), send_sem.at[0], g_recv.at[rdx * 4 + rdz, half], target)

    def g_wait(dx, dz, half):
        await_bytes(g_ref(dx, dz, half), g_recv.at[dx * 4 + dz, half])

    def along_x(dz, half):
        g_push(0, dz, half, x_up, 3, dz)
        g_push(0, dz, half, x_down, 1, dz)

    def pass_up(dz):
        g_wait(3, dz, 0)
        g_push(3, dz, 0, x_up, 2, dz)

    def pass_down(dz):
        g_wait(1, dz, 1)
        g_push(1, dz, 1, x_down, 2, dz)

    g_push(0, 0, 0, z_up, 0, 3)
    g_push(0, 0, 1, z_down, 0, 1)
    g_push(0, 0, 0, x_up, 3, 0)
    g_push(0, 0, 1, x_down, 1, 0)
    g_push(0, 0, 1, x_up, 3, 0)
    g_push(0, 0, 0, x_down, 1, 0)
    kacc[...] = jnp.zeros_like(kacc)
    vacc[...] = jnp.zeros_like(vacc)
    wacc[...] = jnp.zeros_like(wacc)
    kpart[NBLK] = jnp.zeros_like(kpart[NBLK])
    vpart[NBLK] = jnp.zeros_like(vpart[NBLK])

    pass_up(0)
    pass_down(0)
    g_wait(0, 3, 0)
    g_push(0, 3, 0, z_up, 0, 2)
    along_x(3, 0)
    g_wait(0, 1, 1)
    g_push(0, 1, 1, z_down, 0, 2)
    along_x(1, 1)

    for i, (src, dst) in enumerate(((q_in, qh), (k_in, kh), (v_in, vh))):
        @pl.loop(1, NBLK)
        def _(o, i=i, src=src, dst=dst):
            peer = (me + o) % NBLK
            push(src.at[:, columns(peer)], dst.at[me], send_sem.at[1], qkv_recv.at[i], peer)

    for half in range(2):
        g_wait(0, 2, half)
        along_x(2, half)
    pass_up(3)
    pass_down(1)
    pass_up(2)
    pass_down(2)

    for i, dst in enumerate((qh, kh, vh)):
        await_bytes(dst.at[pl.ds(0, NBLK - 1)], qkv_recv.at[i])
    g_push(0, 0, 1, z_up, 0, 3)
    g_push(0, 0, 0, z_down, 0, 1)
    for copy in own:
        copy.wait()

    @pl.loop(0, NBLK)
    def _(b):
        kt[b] = kh[b].T
        vt[b] = vh[b].T

    lane = lax.broadcasted_iota(jnp.int32, (BLOCK, BLOCK), 1)
    sublane = lax.broadcasted_iota(jnp.int32, (BLOCK, BLOCK), 0)

    def forward(b):
        ids = [lists[0, b, j] for j in range(NB)]
        keys = jnp.concatenate([kh[c] for c in ids], axis=0)
        scores = dot(keys, qh[b], NT) * (SCALE * LOG2E)
        query_pos = b * BLOCK + lane
        dead_query = query_pos >= live
        allowed = jnp.concatenate([((c * BLOCK + sublane) < live) | dead_query for c in ids], axis=0)
        scores = jnp.where(allowed, scores, -jnp.inf)
        peak = jnp.max(scores, axis=0, keepdims=True)
        weights = jnp.exp2(scores - peak)
        prob = weights * (1.0 / jnp.sum(weights, axis=0, keepdims=True))
        probs[b] = prob
        values_t = jnp.concatenate([vt[c] for c in ids], axis=1)
        head_t = dot(values_t, prob.astype(BF16), NN)
        heads[b] = jnp.where(dead_query, 0.0, head_t).astype(BF16)

    pl.loop(0, NBLK // 2)(forward)
    g_wait(0, 3, 1)
    along_x(3, 1)
    g_wait(0, 1, 0)
    along_x(1, 0)
    pl.loop(NBLK // 2, NBLK)(forward)

    def backward(slot, b):
        ids = [lists[0, b, j] for j in range(NB)]
        dead_query = (b * BLOCK + lane) >= live
        da_t = jnp.where(dead_query, 0.0, dot(w_ref[...], gall[b], NT)).astype(BF16)
        prob = probs[b]
        grad_prob = dot(jnp.concatenate([vh[c] for c in ids], axis=0), da_t, NN)
        delta = jnp.sum(prob * grad_prob, axis=0, keepdims=True)
        dscore = (prob * (grad_prob - delta) * SCALE).astype(BF16)
        keys_t = jnp.concatenate([kt[c] for c in ids], axis=1)
        dqb[b] = dot(keys_t, dscore, NN).T.astype(BF16)
        at = pl.ds(slot * NB, NB)
        kpart[at] = dot(dscore, qh[b], NN).reshape(NB, BLOCK, HDIM)
        vpart[at] = dot(prob.astype(BF16), da_t, NT).reshape(NB, BLOCK, HDIM)

    def add_parts(blocks):
        ids = [[lists[0, b, j] for j in range(NB)] for b in blocks]

        @pl.loop(0, NBLK)
        def _(c):
            key, value = kacc[c], vacc[c]
            for slot in range(NB):
                place = NBLK
                for j in range(NB):
                    place = jnp.where(ids[slot][j] == c, slot * NB + j, place)
                key = key + kpart[place]
                value = value + vpart[place]
            kacc[c] = key
            vacc[c] = value

    tile = 256

    def add_weight(blocks):
        head = jnp.concatenate([heads[b] for b in blocks], axis=1)

        @pl.loop(0, WIDTH // tile)
        def _(t):
            at = pl.ds(pl.multiple_of(t * tile, tile), tile)
            grad = jnp.concatenate([gall[b, :, at] for b in blocks], axis=0)
            wacc[:, at] += dot(head, grad, NN)

    def send_dq(b):
        push(dqb.at[b], dq_out.at[:, columns(me)], send_sem.at[1], out_recv.at[0], b)

    for dz in (0, 2):
        g_wait(3, dz, 1)
        g_wait(1, dz, 0)
        g_wait(2, dz, 0)
        g_wait(2, dz, 1)

    @pl.loop(0, 2)
    def _(g):
        @pl.loop(0, 4)
        def _(i):
            b = block_at(i, 2 * g)
            backward(i, b)

            @pl.when(g + i > 0)
            def _():
                send_dq(b)

        blocks = [block_at(i, 2 * g) for i in range(4)]
        add_parts(blocks)
        add_weight(blocks)

    pass_down(3)
    pass_up(1)

    for dz in (3, 1):
        g_wait(3, dz, 1)
        g_wait(1, dz, 0)

    @pl.loop(0, 4)
    def _(i):
        b = block_at(3 * (i // 2), 3 - 2 * (i % 2))
        backward(i, b)
        send_dq(b)

    blocks = [block_at(dx, dz) for dx in (0, 3) for dz in (3, 1)]
    add_parts(blocks)
    near, far = [[block_at(dx, dz) for dz in (3, 1)] for dx in (1, 2)]

    @pl.loop(0, 2)
    def _(i):
        b = block_at(1, 3 - 2 * i)
        backward(i, b)
        send_dq(b)

    add_weight(blocks + near)
    for dz in (3, 1):
        g_wait(2, dz, 0)
        g_wait(2, dz, 1)
    add_weight(far)
    wbf[...] = wacc[...].astype(BF16)

    def rows_at(index, size):
        return pl.ds(pl.multiple_of(index * size, size), size)

    push_dp(wbf.at[rows_at(1 - core, HALF)], wcore, send_sem.at[2], w_recv.at[0], other_core)

    @pl.loop(2, 4)
    def _(i):
        b = block_at(2, 7 - 2 * i)
        backward(i, b)
        send_dq(b)

    await_bytes(wcore, w_recv.at[0])
    whalf[...] = wacc[rows_at(core, HALF)] + wcore[...].astype(F32)
    whbf[...] = whalf[...].astype(BF16)
    push_dp(whbf.at[rows_at(1 - low, QUART)], wquart, send_sem.at[3], w_recv.at[1], other_low)

    add_parts(near + far)
    dkb[...] = kacc[...].astype(BF16)
    dvb[...] = vacc[...].astype(BF16)

    @pl.loop(1, NBLK)
    def _(o):
        peer = (me + o) % NBLK
        push(dkb.at[peer], dk_out.at[:, columns(me)], send_sem.at[1], out_recv.at[1], peer)
        push(dvb.at[peer], dv_out.at[:, columns(me)], send_sem.at[1], out_recv.at[2], peer)

    back = [
        pltpu.make_async_copy(src.at[me], dst.at[:, columns(me)], local_sem.at[i])
        for i, (src, dst) in enumerate(((dqb, dq_out), (dkb, dk_out), (dvb, dv_out)))
    ]
    for copy in back:
        copy.start()

    await_bytes(wquart, w_recv.at[1])
    mine = whalf[rows_at(low, QUART)] + wquart[...].astype(F32)
    whalf[pl.ds(0, QUART)] = mine
    wqbf[...] = mine.astype(BF16)

    def piece(index, first=0):
        return (
            pl.ds(pl.multiple_of(first + (index // col_parts) * wrow, wrow), wrow),
            pl.ds(pl.multiple_of((index % col_parts) * wcol, wcol), wcol),
        )

    @pl.loop(1, rows_y)
    def _(o):
        peer = (y + o) % rows_y
        push_dp(wqbf.at[piece(peer)], wrecv.at[o - 1], send_sem.at[4], w_recv.at[2], peer * 4 + scene % 4)

    total = whalf[piece(y)]
    if rows_y > 1:
        await_bytes(wrecv, w_recv.at[2])
        for i in range(rows_y - 1):
            total = total + wrecv[i].astype(F32)
    wres[...] = (total * (1.0 / scenes)).astype(BF16)
    place = dw_out.at[piece(y, core * HALF + low * QUART)]

    @pl.loop(1, rows_y)
    def _(o):
        peer = (y + o) % rows_y
        push_dp(wres, place, send_sem.at[5], w_recv.at[3], peer * 4 + scene % 4)

    keep = pltpu.make_async_copy(wres, place, local_sem.at[3])
    keep.start()
    keep.wait()
    if rows_y > 1:
        await_bytes(wrecv, w_recv.at[3])
    quart = dw_out.at[rows_at(core * 2 + low, QUART)]
    push_dp(quart, quart, send_sem.at[6], w_recv.at[4], other_low)
    await_bytes(wquart, w_recv.at[4])
    half = dw_out.at[rows_at(core, HALF)]
    push_dp(half, half, send_sem.at[7], w_recv.at[5], other_core)

    for copy in back:
        copy.wait()
    for i, out in enumerate((dq_out, dk_out, dv_out)):
        await_bytes(out.at[:, pl.ds(0, WIDTH - HDIM)], out_recv.at[i])
    await_bytes(wcore, w_recv.at[5])
    await_bytes(gall.at[pl.ds(0, NBLK - 1)], send_sem.at[0])
    for dst in (qh, kh, vh, dqb, dkb, dvb):
        await_bytes(dst.at[pl.ds(0, NBLK - 1)], send_sem.at[1])
    await_bytes(wcore, send_sem.at[2])
    await_bytes(wquart, send_sem.at[3])
    if rows_y > 1:
        await_bytes(wrecv, send_sem.at[4])
        await_bytes(wrecv, send_sem.at[5])
    await_bytes(wquart, send_sem.at[6])
    await_bytes(wcore, send_sem.at[7])


def body(queries, keys_in, values, out_grad, out_weight, block_lists, voxel_count):
    scenes = lax.axis_size("dp")
    rows_y = scenes // 4
    row_parts = min(2, rows_y)
    col_parts = rows_y // row_parts
    wrow, wcol = QUART // row_parts, WIDTH // col_parts
    blocks = (NBLK, BLOCK, HDIM)
    hbm = pl.BlockSpec(memory_space=pl.ANY)
    smem = pl.BlockSpec(memory_space=pltpu.SMEM)
    rows = jax.ShapeDtypeStruct((BLOCK, WIDTH), BF16)

    def run(*refs):
        kernel((row_parts, col_parts), *refs)

    return pl.pallas_call(
        run,
        out_shape=(rows, rows, rows, rows),
        in_specs=[hbm, hbm, hbm, hbm, hbm, smem, smem],
        out_specs=(hbm, hbm, hbm, hbm),
        scratch_shapes=[
            pltpu.VMEM(blocks, BF16),
            pltpu.VMEM(blocks, BF16),
            pltpu.VMEM(blocks, BF16),
            pltpu.VMEM(blocks, BF16),
            pltpu.VMEM(blocks, BF16),
            pltpu.VMEM((NBLK, BLOCK, WIDTH), BF16),
            pltpu.VMEM((NBLK, NB * BLOCK, BLOCK), F32),
            pltpu.VMEM(blocks, BF16),
            pltpu.VMEM(blocks, BF16),
            pltpu.VMEM((NBLK + 1, BLOCK, HDIM), F32),
            pltpu.VMEM((NBLK + 1, BLOCK, HDIM), F32),
            pltpu.VMEM(blocks, F32),
            pltpu.VMEM(blocks, F32),
            pltpu.VMEM(blocks, BF16),
            pltpu.VMEM(blocks, BF16),
            pltpu.VMEM((BLOCK, WIDTH), BF16),
            pltpu.VMEM((BLOCK, WIDTH), F32),
            pltpu.VMEM((BLOCK, WIDTH), BF16),
            pltpu.VMEM((HALF, WIDTH), BF16),
            pltpu.VMEM((HALF, WIDTH), F32),
            pltpu.VMEM((HALF, WIDTH), BF16),
            pltpu.VMEM((QUART, WIDTH), BF16),
            pltpu.VMEM((QUART, WIDTH), BF16),
            pltpu.VMEM((max(rows_y - 1, 1), wrow, wcol), BF16),
            pltpu.VMEM((wrow, wcol), BF16),
            pltpu.SemaphoreType.DMA((3,)),
            pltpu.SemaphoreType.DMA((16, 2)),
            pltpu.SemaphoreType.DMA((3,)),
            pltpu.SemaphoreType.DMA((6,)),
            pltpu.SemaphoreType.DMA((8,)),
            pltpu.SemaphoreType.DMA((5,)),
        ],
        compiler_params=pltpu.CompilerParams(
            collective_id=0, has_side_effects=True, vmem_limit_bytes=60 * 1024 * 1024
        ),
        cost_estimate=pl.CostEstimate(flops=4_000_000_000, bytes_accessed=8_000_000, transcendentals=1_000_000),
    )(queries, keys_in, values, out_grad, out_weight, block_lists, voxel_count)


def solution(mesh):
    return jax.shard_map(
        body,
        mesh=mesh,
        in_specs=(
            P(("dp", "shard"), None),
            P(("dp", "shard"), None),
            P(("dp", "shard"), None),
            P(("dp", "shard"), None),
            P("shard", None),
            P("dp", None, None),
            P("dp"),
        ),
        out_specs=(
            P(("dp", "shard"), None),
            P(("dp", "shard"), None),
            P(("dp", "shard"), None),
            P("shard", None),
        ),
        check_vma=False,
    )
```

```python
import math

import jax
import jax.numpy as jnp
from jax import lax
from jax.experimental import pallas as pl
from jax.experimental.pallas import tpu as pltpu
from jax.sharding import PartitionSpec as P

HDIM = 128
BLOCK = 128
NB = 4
NBLK = 16
WIDTH = 2048
HALF = BLOCK // 2
QUART = BLOCK // 4
SCALE = 1.0 / math.sqrt(HDIM)
LOG2E = math.log2(math.e)
F32 = jnp.float32
BF16 = jnp.bfloat16
MESH = pl.DeviceIdType.MESH

NT = (((1,), (1,)), ((), ()))
NN = (((1,), (0,)), ((), ()))


def dot(a, b, dims):
    return lax.dot_general(a, b, dims, preferred_element_type=F32)


def order(i):
    return i + i // 2 - 2 * (i // 3)


def kernel(
    parts,
    q_in, k_in, v_in, g_in, w_in, lists_in, count,
    dq_out, dk_out, dv_out, dw_out,
    qx, kx, vx, qh, kh, vh, kt, vt, gall, probs, heads, dqb, kpart, vpart, kacc, vacc, dkb, dvb,
    w_ref, wacc, wbf, wcore, whalf, whbf, wquart, wqbf, wrecv, wres,
    lists, x_recv, qkv_recv, g_recv, out_recv, w_recv, send_sem, local_sem,
):
    me = lax.axis_index("shard")
    scene = lax.axis_index("dp")
    row_parts, col_parts = parts
    rows_y = row_parts * col_parts
    scenes = 4 * rows_y
    wrow, wcol = QUART // row_parts, WIDTH // col_parts
    core, low, y = scene % 2, (scene // 2) % 2, scene // 4
    x, z = me // 4, me % 4
    x_up, x_down = ((x + 1) % 4) * 4 + z, ((x + 3) % 4) * 4 + z
    z_up, z_down = x * 4 + (z + 1) % 4, x * 4 + (z + 3) % 4
    live = count[0]

    def columns(index):
        return pl.ds(pl.multiple_of(index * HDIM, HDIM), HDIM)

    def heads_of(index):
        return pl.ds(pl.multiple_of(index * 4 * HDIM, 4 * HDIM), 4 * HDIM)

    own = [
        pltpu.make_async_copy(g_in, gall.at[me], local_sem.at[0]),
        pltpu.make_async_copy(q_in.at[:, heads_of(x)], qx.at[x], local_sem.at[1]),
        pltpu.make_async_copy(k_in.at[:, heads_of(x)], kx.at[x], local_sem.at[2]),
        pltpu.make_async_copy(v_in.at[:, heads_of(x)], vx.at[x], local_sem.at[3]),
        pltpu.make_async_copy(w_in, w_ref, local_sem.at[4]),
        pltpu.make_async_copy(lists_in, lists, local_sem.at[5]),
    ]
    for copy in own:
        copy.start()

    barrier = pltpu.get_barrier_semaphore()

    @pl.loop(1, NBLK)
    def _(o):
        pl.semaphore_signal(barrier, inc=1, device_id={"shard": (me + o) % NBLK}, device_id_type=MESH)

    @pl.loop(1, rows_y)
    def _(o):
        pl.semaphore_signal(
            barrier, inc=1, device_id={"dp": ((y + o) % rows_y) * 4 + scene % 4}, device_id_type=MESH
        )

    other_core = scene + 1 - 2 * core
    other_low = scene + 2 - 4 * low
    for peer in (other_core, other_low):
        pl.semaphore_signal(barrier, inc=1, device_id={"dp": peer}, device_id_type=MESH)
    pl.semaphore_wait(barrier, NBLK - 1 + rows_y - 1 + 2)

    def push(src, dst, send, recv, shard):
        pltpu.make_async_remote_copy(
            src_ref=src, dst_ref=dst, send_sem=send, recv_sem=recv,
            device_id={"shard": shard}, device_id_type=MESH,
        ).start()

    def push_dp(src, dst, send, recv, peer):
        pltpu.make_async_remote_copy(
            src_ref=src, dst_ref=dst, send_sem=send, recv_sem=recv,
            device_id={"dp": peer}, device_id_type=MESH,
        ).start()

    def await_bytes(ref, sem):
        pltpu.make_async_copy(ref, ref, sem).wait()

    def block_at(dx, dz):
        return ((x + dx) % 4) * 4 + (z + dz) % 4

    def g_ref(dx, dz, half):
        return gall.at[block_at(dx, dz), pl.ds(half * HALF, HALF)]

    def g_push(dx, dz, half, target, rdx, rdz):
        src = g_in.at[pl.ds(half * HALF, HALF)] if (dx, dz) == (0, 0) else g_ref(dx, dz, half)
        push(src, g_ref(dx, dz, half), send_sem.at[0], g_recv.at[rdx * 4 + rdz, half], target)

    def g_wait(dx, dz, half):
        await_bytes(g_ref(dx, dz, half), g_recv.at[dx * 4 + dz, half])

    def along_x(dz, half):
        g_push(0, dz, half, x_up, 3, dz)
        g_push(0, dz, half, x_down, 1, dz)

    def pass_up(dz):
        g_wait(3, dz, 0)
        g_push(3, dz, 0, x_up, 2, dz)

    def pass_down(dz):
        g_wait(1, dz, 1)
        g_push(1, dz, 1, x_down, 2, dz)

    arrays = ((q_in, qx, qh), (k_in, kx, kh), (v_in, vx, vh))
    for i, (src, mid, dst) in enumerate(arrays):
        for o in (1, 3, 2):
            to_x = (x + o) % 4
            push(src.at[:, heads_of(to_x)], mid.at[x], send_sem.at[8], x_recv.at[i], to_x * 4 + z)

    g_push(0, 0, 0, z_up, 0, 3)
    g_push(0, 0, 1, z_down, 0, 1)
    g_push(0, 0, 0, x_up, 3, 0)
    g_push(0, 0, 1, x_down, 1, 0)
    g_push(0, 0, 1, x_up, 3, 0)
    g_push(0, 0, 0, x_down, 1, 0)
    kacc[...] = jnp.zeros_like(kacc)
    vacc[...] = jnp.zeros_like(vacc)
    wacc[...] = jnp.zeros_like(wacc)
    kpart[NBLK] = jnp.zeros_like(kpart[NBLK])
    vpart[NBLK] = jnp.zeros_like(vpart[NBLK])
    for copy in own:
        copy.wait()

    def along_z(i):
        src, mid, dst = arrays[i]
        await_bytes(mid.at[pl.ds(0, 3)], x_recv.at[i])
        for o in (1, 3, 2):
            to_z = (z + o) % 4
            push(mid.at[:, :, columns(to_z)], dst.at[:, z], send_sem.at[8], qkv_recv.at[i], x * 4 + to_z)
        pltpu.make_async_copy(mid.at[:, :, columns(z)], dst.at[:, z], local_sem.at[i]).start()

    g_wait(0, 3, 0)
    g_push(0, 3, 0, z_up, 0, 2)
    along_x(3, 0)
    g_wait(0, 1, 1)
    g_push(0, 1, 1, z_down, 0, 2)
    along_x(1, 1)
    for i in range(3):
        along_z(i)
    pass_up(0)
    pass_down(0)
    for half in range(2):
        g_wait(0, 2, half)
        along_x(2, half)
    pass_up(3)
    pass_down(1)
    pass_up(2)
    pass_down(2)

    g_push(0, 0, 1, z_up, 0, 3)
    g_push(0, 0, 0, z_down, 0, 1)
    for i, (src, mid, dst) in enumerate(arrays):
        await_bytes(dst.at[pl.ds(0, 3)], qkv_recv.at[i])
        pltpu.make_async_copy(mid.at[:, :, columns(z)], dst.at[:, z], local_sem.at[i]).wait()

    @pl.loop(0, NBLK)
    def _(b):
        kt[b] = kh[b // 4, b % 4].T
        vt[b] = vh[b // 4, b % 4].T

    lane = lax.broadcasted_iota(jnp.int32, (BLOCK, BLOCK), 1)
    sublane = lax.broadcasted_iota(jnp.int32, (BLOCK, BLOCK), 0)

    def forward(b):
        ids = [lists[0, j, b] for j in range(NB)]
        keys = jnp.concatenate([kh[c // 4, c % 4] for c in ids], axis=0)
        scores = dot(keys, qh[b // 4, b % 4], NT) * (SCALE * LOG2E)
        query_pos = b * BLOCK + lane
        dead_query = query_pos >= live
        allowed = jnp.concatenate([((c * BLOCK + sublane) < live) | dead_query for c in ids], axis=0)
        scores = jnp.where(allowed, scores, -jnp.inf)
        peak = jnp.max(scores, axis=0, keepdims=True)
        weights = jnp.exp2(scores - peak)
        prob = weights * (1.0 / jnp.sum(weights, axis=0, keepdims=True))
        probs[b] = prob
        values_t = jnp.concatenate([vt[c] for c in ids], axis=1)
        head_t = dot(values_t, prob.astype(BF16), NN)
        heads[b] = jnp.where(dead_query, 0.0, head_t).astype(BF16)

    pl.loop(0, NBLK // 2)(forward)
    g_wait(0, 3, 1)
    along_x(3, 1)
    g_wait(0, 1, 0)
    along_x(1, 0)
    pl.loop(NBLK // 2, NBLK)(forward)

    def backward(slot, b):
        ids = [lists[0, j, b] for j in range(NB)]
        dead_query = (b * BLOCK + lane) >= live
        da_t = jnp.where(dead_query, 0.0, dot(w_ref[...], gall[b], NT)).astype(BF16)
        prob = probs[b]
        grad_prob = dot(jnp.concatenate([vh[c // 4, c % 4] for c in ids], axis=0), da_t, NN)
        delta = jnp.sum(prob * grad_prob, axis=0, keepdims=True)
        dscore = (prob * (grad_prob - delta) * SCALE).astype(BF16)
        keys_t = jnp.concatenate([kt[c] for c in ids], axis=1)
        dqb[b] = dot(keys_t, dscore, NN).T.astype(BF16)
        at = pl.ds(slot * NB, NB)
        kpart[at] = dot(dscore, qh[b // 4, b % 4], NN).reshape(NB, BLOCK, HDIM)
        vpart[at] = dot(prob.astype(BF16), da_t, NT).reshape(NB, BLOCK, HDIM)

    def add_parts(blocks):
        ids = [[lists[0, j, b] for j in range(NB)] for b in blocks]

        @pl.loop(0, NBLK)
        def _(c):
            key, value = kacc[c], vacc[c]
            for slot in range(NB):
                place = NBLK
                for j in range(NB):
                    place = jnp.where(ids[slot][j] == c, slot * NB + j, place)
                key = key + kpart[place]
                value = value + vpart[place]
            kacc[c] = key
            vacc[c] = value

    tile = 256

    def add_weight(blocks):
        head = jnp.concatenate([heads[b] for b in blocks], axis=1)

        @pl.loop(0, WIDTH // tile)
        def _(t):
            at = pl.ds(pl.multiple_of(t * tile, tile), tile)
            grad = jnp.concatenate([gall[b, :, at] for b in blocks], axis=0)
            wacc[:, at] += dot(head, grad, NN)

    def send_dq(b):
        push(dqb.at[b], dq_out.at[:, columns(me)], send_sem.at[1], out_recv.at[0], b)

    for dz in (0, 2):
        g_wait(3, dz, 1)
        g_wait(1, dz, 0)
        g_wait(2, dz, 0)
        g_wait(2, dz, 1)

    @pl.loop(0, 2)
    def _(g):
        @pl.loop(0, 4)
        def _(i):
            b = block_at(i, 2 * g)
            backward(i, b)

            @pl.when(g + i > 0)
            def _():
                send_dq(b)

        blocks = [block_at(i, 2 * g) for i in range(4)]
        add_parts(blocks)
        add_weight(blocks)

    pass_down(3)
    pass_up(1)

    for dz in (3, 1):
        g_wait(3, dz, 1)
        g_wait(1, dz, 0)

    @pl.loop(0, 4)
    def _(i):
        b = block_at(3 * (i // 2), 3 - 2 * (i % 2))
        backward(i, b)
        send_dq(b)

    blocks = [block_at(dx, dz) for dx in (0, 3) for dz in (3, 1)]
    add_parts(blocks)
    near, far = [[block_at(dx, dz) for dz in (3, 1)] for dx in (1, 2)]

    @pl.loop(0, 2)
    def _(i):
        b = block_at(1, 3 - 2 * i)
        backward(i, b)
        send_dq(b)

    add_weight(blocks + near)
    for dz in (3, 1):
        g_wait(2, dz, 0)
        g_wait(2, dz, 1)
    add_weight(far)
    wbf[...] = wacc[...].astype(BF16)

    def rows_at(index, size):
        return pl.ds(pl.multiple_of(index * size, size), size)

    push_dp(wbf.at[rows_at(1 - core, HALF)], wcore, send_sem.at[2], w_recv.at[0], other_core)

    @pl.loop(2, 4)
    def _(i):
        b = block_at(2, 7 - 2 * i)
        backward(i, b)
        send_dq(b)

    await_bytes(wcore, w_recv.at[0])
    whalf[...] = wacc[rows_at(core, HALF)] + wcore[...].astype(F32)
    whbf[...] = whalf[...].astype(BF16)
    push_dp(whbf.at[rows_at(1 - low, QUART)], wquart, send_sem.at[3], w_recv.at[1], other_low)

    add_parts(near + far)
    dkb[...] = kacc[...].astype(BF16)
    dvb[...] = vacc[...].astype(BF16)

    @pl.loop(1, NBLK)
    def _(o):
        peer = (me + o) % NBLK
        push(dkb.at[peer], dk_out.at[:, columns(me)], send_sem.at[1], out_recv.at[1], peer)
        push(dvb.at[peer], dv_out.at[:, columns(me)], send_sem.at[1], out_recv.at[2], peer)

    back = [
        pltpu.make_async_copy(src.at[me], dst.at[:, columns(me)], local_sem.at[i])
        for i, (src, dst) in enumerate(((dqb, dq_out), (dkb, dk_out), (dvb, dv_out)))
    ]
    for copy in back:
        copy.start()

    await_bytes(wquart, w_recv.at[1])
    mine = whalf[rows_at(low, QUART)] + wquart[...].astype(F32)
    whalf[pl.ds(0, QUART)] = mine
    wqbf[...] = mine.astype(BF16)

    def piece(index, first=0):
        return (
            pl.ds(pl.multiple_of(first + (index // col_parts) * wrow, wrow), wrow),
            pl.ds(pl.multiple_of((index % col_parts) * wcol, wcol), wcol),
        )

    @pl.loop(1, rows_y)
    def _(o):
        peer = (y + o) % rows_y
        push_dp(wqbf.at[piece(peer)], wrecv.at[o - 1], send_sem.at[4], w_recv.at[2], peer * 4 + scene % 4)

    total = whalf[piece(y)]
    if rows_y > 1:
        await_bytes(wrecv, w_recv.at[2])
        for i in range(rows_y - 1):
            total = total + wrecv[i].astype(F32)
    wres[...] = (total * (1.0 / scenes)).astype(BF16)
    place = dw_out.at[piece(y, core * HALF + low * QUART)]

    @pl.loop(1, rows_y)
    def _(o):
        peer = (y + o) % rows_y
        push_dp(wres, place, send_sem.at[5], w_recv.at[3], peer * 4 + scene % 4)

    keep = pltpu.make_async_copy(wres, place, local_sem.at[3])
    keep.start()
    keep.wait()
    if rows_y > 1:
        await_bytes(wrecv, w_recv.at[3])
    quart = dw_out.at[rows_at(core * 2 + low, QUART)]
    push_dp(quart, quart, send_sem.at[6], w_recv.at[4], other_low)
    await_bytes(wquart, w_recv.at[4])
    half = dw_out.at[rows_at(core, HALF)]
    push_dp(half, half, send_sem.at[7], w_recv.at[5], other_core)

    for copy in back:
        copy.wait()
    for i, out in enumerate((dq_out, dk_out, dv_out)):
        await_bytes(out.at[:, pl.ds(0, WIDTH - HDIM)], out_recv.at[i])
    await_bytes(wcore, w_recv.at[5])
    await_bytes(gall.at[pl.ds(0, NBLK - 1)], send_sem.at[0])
    for dst in (dqb, dkb, dvb):
        await_bytes(dst.at[pl.ds(0, NBLK - 1)], send_sem.at[1])
    for mid in (qx, kx, vx, qx, kx, vx):
        await_bytes(mid.at[pl.ds(0, 3)], send_sem.at[8])
    await_bytes(wcore, send_sem.at[2])
    await_bytes(wquart, send_sem.at[3])
    if rows_y > 1:
        await_bytes(wrecv, send_sem.at[4])
        await_bytes(wrecv, send_sem.at[5])
    await_bytes(wquart, send_sem.at[6])
    await_bytes(wcore, send_sem.at[7])


def body(queries, keys_in, values, out_grad, out_weight, block_lists, voxel_count):
    scenes = lax.axis_size("dp")
    rows_y = scenes // 4
    row_parts = min(2, rows_y)
    col_parts = rows_y // row_parts
    wrow, wcol = QUART // row_parts, WIDTH // col_parts
    blocks = (NBLK, BLOCK, HDIM)
    hbm = pl.BlockSpec(memory_space=pl.ANY)
    smem = pl.BlockSpec(memory_space=pltpu.SMEM)
    rows = jax.ShapeDtypeStruct((BLOCK, WIDTH), BF16)

    def run(*refs):
        kernel((row_parts, col_parts), *refs)

    grads = pl.pallas_call(
        run,
        out_shape=(rows, rows, rows, rows),
        in_specs=[hbm, hbm, hbm, hbm, hbm, hbm, smem],
        out_specs=(hbm, hbm, hbm, hbm),
        scratch_shapes=[
            pltpu.VMEM((4, BLOCK, 4 * HDIM), BF16),
            pltpu.VMEM((4, BLOCK, 4 * HDIM), BF16),
            pltpu.VMEM((4, BLOCK, 4 * HDIM), BF16),
            pltpu.VMEM((4, 4, BLOCK, HDIM), BF16),
            pltpu.VMEM((4, 4, BLOCK, HDIM), BF16),
            pltpu.VMEM((4, 4, BLOCK, HDIM), BF16),
            pltpu.VMEM(blocks, BF16),
            pltpu.VMEM(blocks, BF16),
            pltpu.VMEM((NBLK, BLOCK, WIDTH), BF16),
            pltpu.VMEM((NBLK, NB * BLOCK, BLOCK), F32),
            pltpu.VMEM(blocks, BF16),
            pltpu.VMEM(blocks, BF16),
            pltpu.VMEM((NBLK + 1, BLOCK, HDIM), F32),
            pltpu.VMEM((NBLK + 1, BLOCK, HDIM), F32),
            pltpu.VMEM(blocks, F32),
            pltpu.VMEM(blocks, F32),
            pltpu.VMEM(blocks, BF16),
            pltpu.VMEM(blocks, BF16),
            pltpu.VMEM((BLOCK, WIDTH), BF16),
            pltpu.VMEM((BLOCK, WIDTH), F32),
            pltpu.VMEM((BLOCK, WIDTH), BF16),
            pltpu.VMEM((HALF, WIDTH), BF16),
            pltpu.VMEM((HALF, WIDTH), F32),
            pltpu.VMEM((HALF, WIDTH), BF16),
            pltpu.VMEM((QUART, WIDTH), BF16),
            pltpu.VMEM((QUART, WIDTH), BF16),
            pltpu.VMEM((max(rows_y - 1, 1), wrow, wcol), BF16),
            pltpu.VMEM((wrow, wcol), BF16),
            pltpu.SMEM((1, NB, NBLK), jnp.int32),
            pltpu.SemaphoreType.DMA((3,)),
            pltpu.SemaphoreType.DMA((3,)),
            pltpu.SemaphoreType.DMA((16, 2)),
            pltpu.SemaphoreType.DMA((3,)),
            pltpu.SemaphoreType.DMA((6,)),
            pltpu.SemaphoreType.DMA((9,)),
            pltpu.SemaphoreType.DMA((6,)),
        ],
        compiler_params=pltpu.CompilerParams(
            collective_id=0, has_side_effects=True, vmem_limit_bytes=60 * 1024 * 1024
        ),
        cost_estimate=pl.CostEstimate(flops=4_000_000_000, bytes_accessed=8_000_000, transcendentals=1_000_000),
    )(queries, keys_in, values, out_grad, out_weight, jnp.transpose(block_lists, (0, 2, 1)), voxel_count)

    def hand_over(*refs):
        ins, outs, held, sems = refs[:4], refs[4:8], refs[8], refs[9]
        reads = [pltpu.make_async_copy(src, held.at[i], sems.at[0, i]) for i, src in enumerate(ins)]
        writes = [pltpu.make_async_copy(held.at[i], dst, sems.at[1, i]) for i, dst in enumerate(outs)]
        for copy in reads:
            copy.start()
        for read, write in zip(reads, writes):
            read.wait()
            write.start()
        for copy in writes:
            copy.wait()

    return pl.pallas_call(
        hand_over,
        out_shape=(rows, rows, rows, rows),
        in_specs=[hbm] * 4,
        out_specs=(hbm,) * 4,
        scratch_shapes=[pltpu.VMEM((4, BLOCK, WIDTH), BF16), pltpu.SemaphoreType.DMA((2, 4))],
        compiler_params=pltpu.CompilerParams(vmem_limit_bytes=60 * 1024 * 1024),
    )(*grads)


def solution(mesh):
    return jax.shard_map(
        body,
        mesh=mesh,
        in_specs=(
            P(("dp", "shard"), None),
            P(("dp", "shard"), None),
            P(("dp", "shard"), None),
            P(("dp", "shard"), None),
            P("shard", None),
            P("dp", None, None),
            P("dp"),
        ),
        out_specs=(
            P(("dp", "shard"), None),
            P(("dp", "shard"), None),
            P(("dp", "shard"), None),
            P("shard", None),
        ),
        check_vma=False,
    )
```

```python
import math

import jax
import jax.numpy as jnp
from jax import lax
from jax.experimental import pallas as pl
from jax.experimental.pallas import tpu as pltpu
from jax.sharding import PartitionSpec as P

HDIM = 128
BLOCK = 128
NB = 4
NBLK = 16
WIDTH = 2048
HALF = BLOCK // 2
QUART = BLOCK // 4
SCALE = 1.0 / math.sqrt(HDIM)
LOG2E = math.log2(math.e)
F32 = jnp.float32
BF16 = jnp.bfloat16
MESH = pl.DeviceIdType.MESH

NT = (((1,), (1,)), ((), ()))
NN = (((1,), (0,)), ((), ()))


def dot(a, b, dims):
    return lax.dot_general(a, b, dims, preferred_element_type=F32)


def order(i):
    return i + i // 2 - 2 * (i // 3)


def kernel(
    parts,
    q_in, k_in, v_in, g_in, w_in, lists_in, count,
    dq_out, dk_out, dv_out, dw_out,
    da, qx, kx, vx, qh, kh, vh, kt, vt, gall, probs, heads, dqb, kpart, vpart, kacc, vacc, dkb, dvb,
    w_ref, wacc, wbf, wcore, whalf, whbf, wquart, wqbf, wrecv, wres,
    lists, x_recv, qkv_recv, g_recv, out_recv, w_recv, send_sem, local_sem,
):
    me = lax.axis_index("shard")
    scene = lax.axis_index("dp")
    row_parts, col_parts = parts
    rows_y = row_parts * col_parts
    scenes = 4 * rows_y
    wrow, wcol = QUART // row_parts, WIDTH // col_parts
    core, low, y = scene % 2, (scene // 2) % 2, scene // 4
    x, z = me // 4, me % 4
    x_up, x_down = ((x + 1) % 4) * 4 + z, ((x + 3) % 4) * 4 + z
    z_up, z_down = x * 4 + (z + 1) % 4, x * 4 + (z + 3) % 4
    live = count[0]

    def columns(index):
        return pl.ds(pl.multiple_of(index * HDIM, HDIM), HDIM)

    def heads_of(index):
        return pl.ds(pl.multiple_of(index * 4 * HDIM, 4 * HDIM), 4 * HDIM)

    own = [
        pltpu.make_async_copy(g_in, gall.at[me], local_sem.at[0]),
        pltpu.make_async_copy(q_in.at[:, heads_of(x)], qx.at[x], local_sem.at[1]),
        pltpu.make_async_copy(k_in.at[:, heads_of(x)], kx.at[x], local_sem.at[2]),
        pltpu.make_async_copy(v_in.at[:, heads_of(x)], vx.at[x], local_sem.at[3]),
        pltpu.make_async_copy(w_in, w_ref, local_sem.at[4]),
        pltpu.make_async_copy(lists_in, lists, local_sem.at[5]),
    ]
    for copy in own:
        copy.start()

    barrier = pltpu.get_barrier_semaphore()

    @pl.loop(1, NBLK)
    def _(o):
        pl.semaphore_signal(barrier, inc=1, device_id={"shard": (me + o) % NBLK}, device_id_type=MESH)

    @pl.loop(1, rows_y)
    def _(o):
        pl.semaphore_signal(
            barrier, inc=1, device_id={"dp": ((y + o) % rows_y) * 4 + scene % 4}, device_id_type=MESH
        )

    other_core = scene + 1 - 2 * core
    other_low = scene + 2 - 4 * low
    for peer in (other_core, other_low):
        pl.semaphore_signal(barrier, inc=1, device_id={"dp": peer}, device_id_type=MESH)
    pl.semaphore_wait(barrier, NBLK - 1 + rows_y - 1 + 2)

    def push(src, dst, send, recv, shard):
        pltpu.make_async_remote_copy(
            src_ref=src, dst_ref=dst, send_sem=send, recv_sem=recv,
            device_id={"shard": shard}, device_id_type=MESH,
        ).start()

    def push_dp(src, dst, send, recv, peer):
        pltpu.make_async_remote_copy(
            src_ref=src, dst_ref=dst, send_sem=send, recv_sem=recv,
            device_id={"dp": peer}, device_id_type=MESH,
        ).start()

    def await_bytes(ref, sem):
        pltpu.make_async_copy(ref, ref, sem).wait()

    def block_at(dx, dz):
        return ((x + dx) % 4) * 4 + (z + dz) % 4

    def g_ref(dx, dz, half):
        return gall.at[block_at(dx, dz), pl.ds(half * HALF, HALF)]

    def g_push(dx, dz, half, target, rdx, rdz):
        src = g_in.at[pl.ds(half * HALF, HALF)] if (dx, dz) == (0, 0) else g_ref(dx, dz, half)
        push(src, g_ref(dx, dz, half), send_sem.at[0], g_recv.at[rdx * 4 + rdz, half], target)

    def g_wait(dx, dz, half):
        await_bytes(g_ref(dx, dz, half), g_recv.at[dx * 4 + dz, half])

    def along_x(dz, half):
        g_push(0, dz, half, x_up, 3, dz)
        g_push(0, dz, half, x_down, 1, dz)

    def pass_up(dz):
        g_wait(3, dz, 0)
        g_push(3, dz, 0, x_up, 2, dz)

    def pass_down(dz):
        g_wait(1, dz, 1)
        g_push(1, dz, 1, x_down, 2, dz)

    arrays = ((q_in, qx, qh), (k_in, kx, kh), (v_in, vx, vh))
    for i, (src, mid, dst) in enumerate(arrays):
        for o in (1, 3, 2):
            to_x = (x + o) % 4
            push(src.at[:, heads_of(to_x)], mid.at[x], send_sem.at[8], x_recv.at[i], to_x * 4 + z)

    g_push(0, 0, 0, z_up, 0, 3)
    g_push(0, 0, 1, z_down, 0, 1)
    g_push(0, 0, 0, x_up, 3, 0)
    g_push(0, 0, 1, x_down, 1, 0)
    g_push(0, 0, 1, x_up, 3, 0)
    g_push(0, 0, 0, x_down, 1, 0)
    kacc[...] = jnp.zeros_like(kacc)
    vacc[...] = jnp.zeros_like(vacc)
    wacc[...] = jnp.zeros_like(wacc)
    kpart[NBLK] = jnp.zeros_like(kpart[NBLK])
    vpart[NBLK] = jnp.zeros_like(vpart[NBLK])
    for copy in own:
        copy.wait()

    def along_z(i):
        src, mid, dst = arrays[i]
        await_bytes(mid.at[pl.ds(0, 3)], x_recv.at[i])
        for o in (1, 3, 2):
            to_z = (z + o) % 4
            push(mid.at[:, :, columns(to_z)], dst.at[:, z], send_sem.at[8], qkv_recv.at[i], x * 4 + to_z)
        pltpu.make_async_copy(mid.at[:, :, columns(z)], dst.at[:, z], local_sem.at[i]).start()

    g_wait(0, 3, 0)
    g_push(0, 3, 0, z_up, 0, 2)
    along_x(3, 0)
    g_wait(0, 1, 1)
    g_push(0, 1, 1, z_down, 0, 2)
    along_x(1, 1)
    for i in range(3):
        along_z(i)
    pass_up(0)
    pass_down(0)
    for half in range(2):
        g_wait(0, 2, half)
        along_x(2, half)
    pass_up(3)
    pass_down(1)
    pass_up(2)
    pass_down(2)

    g_push(0, 0, 1, z_up, 0, 3)
    g_push(0, 0, 0, z_down, 0, 1)
    lane = lax.broadcasted_iota(jnp.int32, (BLOCK, BLOCK), 1)
    sublane = lax.broadcasted_iota(jnp.int32, (BLOCK, BLOCK), 0)

    def grad_attn(b):
        dead_query = (b * BLOCK + lane) >= live
        return jnp.where(dead_query, 0.0, dot(w_ref[...], gall[b], NT)).astype(BF16)

    g_wait(3, 0, 1)
    g_wait(1, 0, 0)
    g_wait(2, 0, 0)
    g_wait(2, 0, 1)

    @pl.loop(0, 4)
    def _(i):
        b = block_at(i, 0)
        da[b] = grad_attn(b)

    for i, (src, mid, dst) in enumerate(arrays):
        await_bytes(dst.at[pl.ds(0, 3)], qkv_recv.at[i])
        pltpu.make_async_copy(mid.at[:, :, columns(z)], dst.at[:, z], local_sem.at[i]).wait()

    @pl.loop(0, NBLK)
    def _(b):
        kt[b] = kh[b // 4, b % 4].T
        vt[b] = vh[b // 4, b % 4].T

    def forward(b):
        ids = [lists[0, j, b] for j in range(NB)]
        keys = jnp.concatenate([kh[c // 4, c % 4] for c in ids], axis=0)
        scores = dot(keys, qh[b // 4, b % 4], NT) * (SCALE * LOG2E)
        query_pos = b * BLOCK + lane
        dead_query = query_pos >= live
        allowed = jnp.concatenate([((c * BLOCK + sublane) < live) | dead_query for c in ids], axis=0)
        scores = jnp.where(allowed, scores, -jnp.inf)
        peak = jnp.max(scores, axis=0, keepdims=True)
        weights = jnp.exp2(scores - peak)
        prob = weights * (1.0 / jnp.sum(weights, axis=0, keepdims=True))
        probs[b] = prob
        values_t = jnp.concatenate([vt[c] for c in ids], axis=1)
        head_t = dot(values_t, prob.astype(BF16), NN)
        heads[b] = jnp.where(dead_query, 0.0, head_t).astype(BF16)

    pl.loop(0, NBLK // 2, unroll=2)(forward)
    g_wait(0, 3, 1)
    along_x(3, 1)
    g_wait(0, 1, 0)
    along_x(1, 0)
    pl.loop(NBLK // 2, NBLK, unroll=2)(forward)

    def backward(slot, b, early=False):
        ids = [lists[0, j, b] for j in range(NB)]
        da_t = da[b] if early else grad_attn(b)
        prob = probs[b]
        grad_prob = dot(jnp.concatenate([vh[c // 4, c % 4] for c in ids], axis=0), da_t, NN)
        delta = jnp.sum(prob * grad_prob, axis=0, keepdims=True)
        dscore = (prob * (grad_prob - delta) * SCALE).astype(BF16)
        keys_t = jnp.concatenate([kt[c] for c in ids], axis=1)
        dqb[b] = dot(keys_t, dscore, NN).T.astype(BF16)
        at = pl.ds(slot * NB, NB)
        kpart[at] = dot(dscore, qh[b // 4, b % 4], NN).reshape(NB, BLOCK, HDIM)
        vpart[at] = dot(prob.astype(BF16), da_t, NT).reshape(NB, BLOCK, HDIM)

    def add_parts(blocks):
        ids = [[lists[0, j, b] for j in range(NB)] for b in blocks]

        @pl.loop(0, NBLK)
        def _(c):
            key, value = kacc[c], vacc[c]
            for slot in range(NB):
                place = NBLK
                for j in range(NB):
                    place = jnp.where(ids[slot][j] == c, slot * NB + j, place)
                key = key + kpart[place]
                value = value + vpart[place]
            kacc[c] = key
            vacc[c] = value

    tile = 256

    def add_weight(blocks):
        head = jnp.concatenate([heads[b] for b in blocks], axis=1)

        @pl.loop(0, WIDTH // tile)
        def _(t):
            at = pl.ds(pl.multiple_of(t * tile, tile), tile)
            grad = jnp.concatenate([gall[b, :, at] for b in blocks], axis=0)
            wacc[:, at] += dot(head, grad, NN)

    def send_dq(b):
        push(dqb.at[b], dq_out.at[:, columns(me)], send_sem.at[1], out_recv.at[0], b)

    for dz in (2,):
        g_wait(3, dz, 1)
        g_wait(1, dz, 0)
        g_wait(2, dz, 0)
        g_wait(2, dz, 1)

    for dz in (0, 2):
        @pl.loop(0, 4, step=2)
        def _(i, dz=dz):
            for j in range(2):
                backward(i + j, block_at(i + j, dz), early=dz == 0)

            @pl.when(dz + i > 0)
            def _():
                send_dq(block_at(i, dz))

            send_dq(block_at(i + 1, dz))

        blocks = [block_at(dx, dz) for dx in range(4)]
        add_parts(blocks)
        add_weight(blocks)

    pass_down(3)
    pass_up(1)

    for dz in (3, 1):
        g_wait(3, dz, 1)
        g_wait(1, dz, 0)

    @pl.loop(0, 2)
    def _(i):
        pair = [block_at(3 * i, dz) for dz in (3, 1)]
        for j in range(2):
            backward(2 * i + j, pair[j])
        for b in pair:
            send_dq(b)

    blocks = [block_at(dx, dz) for dx in (0, 3) for dz in (3, 1)]
    add_parts(blocks)
    near, far = [[block_at(dx, dz) for dz in (3, 1)] for dx in (1, 2)]

    for i in range(2):
        backward(i, near[i])
    for b in near:
        send_dq(b)

    add_weight(blocks + near)
    for dz in (3, 1):
        g_wait(2, dz, 0)
        g_wait(2, dz, 1)
    add_weight(far)
    wbf[...] = wacc[...].astype(BF16)

    def rows_at(index, size):
        return pl.ds(pl.multiple_of(index * size, size), size)

    push_dp(wbf.at[rows_at(1 - core, HALF)], wcore, send_sem.at[2], w_recv.at[0], other_core)

    for i in range(2):
        backward(2 + i, far[i])
    for b in far:
        send_dq(b)

    await_bytes(wcore, w_recv.at[0])
    whalf[...] = wacc[rows_at(core, HALF)] + wcore[...].astype(F32)
    whbf[...] = whalf[...].astype(BF16)
    push_dp(whbf.at[rows_at(1 - low, QUART)], wquart, send_sem.at[3], w_recv.at[1], other_low)

    add_parts(near + far)
    dkb[...] = kacc[...].astype(BF16)
    dvb[...] = vacc[...].astype(BF16)

    @pl.loop(1, NBLK)
    def _(o):
        peer = (me + o) % NBLK
        push(dkb.at[peer], dk_out.at[:, columns(me)], send_sem.at[1], out_recv.at[1], peer)
        push(dvb.at[peer], dv_out.at[:, columns(me)], send_sem.at[1], out_recv.at[2], peer)

    back = [
        pltpu.make_async_copy(src.at[me], dst.at[:, columns(me)], local_sem.at[i])
        for i, (src, dst) in enumerate(((dqb, dq_out), (dkb, dk_out), (dvb, dv_out)))
    ]
    for copy in back:
        copy.start()

    await_bytes(wquart, w_recv.at[1])
    mine = whalf[rows_at(low, QUART)] + wquart[...].astype(F32)
    whalf[pl.ds(0, QUART)] = mine
    wqbf[...] = mine.astype(BF16)

    def piece(index, first=0):
        return (
            pl.ds(pl.multiple_of(first + (index // col_parts) * wrow, wrow), wrow),
            pl.ds(pl.multiple_of((index % col_parts) * wcol, wcol), wcol),
        )

    @pl.loop(1, rows_y)
    def _(o):
        peer = (y + o) % rows_y
        push_dp(wqbf.at[piece(peer)], wrecv.at[o - 1], send_sem.at[4], w_recv.at[2], peer * 4 + scene % 4)

    total = whalf[piece(y)]
    if rows_y > 1:
        await_bytes(wrecv, w_recv.at[2])
        for i in range(rows_y - 1):
            total = total + wrecv[i].astype(F32)
    wres[...] = (total * (1.0 / scenes)).astype(BF16)
    place = dw_out.at[piece(y, core * HALF + low * QUART)]

    @pl.loop(1, rows_y)
    def _(o):
        peer = (y + o) % rows_y
        push_dp(wres, place, send_sem.at[5], w_recv.at[3], peer * 4 + scene % 4)

    keep = pltpu.make_async_copy(wres, place, local_sem.at[3])
    keep.start()
    keep.wait()
    if rows_y > 1:
        await_bytes(wrecv, w_recv.at[3])
    quart = dw_out.at[rows_at(core * 2 + low, QUART)]
    push_dp(quart, quart, send_sem.at[6], w_recv.at[4], other_low)
    await_bytes(wquart, w_recv.at[4])
    half = dw_out.at[rows_at(core, HALF)]
    push_dp(half, half, send_sem.at[7], w_recv.at[5], other_core)

    for copy in back:
        copy.wait()
    for i, out in enumerate((dq_out, dk_out, dv_out)):
        await_bytes(out.at[:, pl.ds(0, WIDTH - HDIM)], out_recv.at[i])
    await_bytes(wcore, w_recv.at[5])
    await_bytes(gall.at[pl.ds(0, NBLK - 1)], send_sem.at[0])
    for dst in (dqb, dkb, dvb):
        await_bytes(dst.at[pl.ds(0, NBLK - 1)], send_sem.at[1])
    for mid in (qx, kx, vx, qx, kx, vx):
        await_bytes(mid.at[pl.ds(0, 3)], send_sem.at[8])
    await_bytes(wcore, send_sem.at[2])
    await_bytes(wquart, send_sem.at[3])
    if rows_y > 1:
        await_bytes(wrecv, send_sem.at[4])
        await_bytes(wrecv, send_sem.at[5])
    await_bytes(wquart, send_sem.at[6])
    await_bytes(wcore, send_sem.at[7])


def body(queries, keys_in, values, out_grad, out_weight, block_lists, voxel_count):
    scenes = lax.axis_size("dp")
    rows_y = scenes // 4
    row_parts = min(2, rows_y)
    col_parts = rows_y // row_parts
    wrow, wcol = QUART // row_parts, WIDTH // col_parts
    blocks = (NBLK, BLOCK, HDIM)
    hbm = pl.BlockSpec(memory_space=pl.ANY)
    smem = pl.BlockSpec(memory_space=pltpu.SMEM)
    rows = jax.ShapeDtypeStruct((BLOCK, WIDTH), BF16)

    def run(*refs):
        kernel((row_parts, col_parts), *refs)

    grads = pl.pallas_call(
        run,
        out_shape=(rows, rows, rows, rows),
        in_specs=[hbm, hbm, hbm, hbm, hbm, hbm, smem],
        out_specs=(hbm, hbm, hbm, hbm),
        scratch_shapes=[
            pltpu.VMEM(blocks, BF16),
            pltpu.VMEM((4, BLOCK, 4 * HDIM), BF16),
            pltpu.VMEM((4, BLOCK, 4 * HDIM), BF16),
            pltpu.VMEM((4, BLOCK, 4 * HDIM), BF16),
            pltpu.VMEM((4, 4, BLOCK, HDIM), BF16),
            pltpu.VMEM((4, 4, BLOCK, HDIM), BF16),
            pltpu.VMEM((4, 4, BLOCK, HDIM), BF16),
            pltpu.VMEM(blocks, BF16),
            pltpu.VMEM(blocks, BF16),
            pltpu.VMEM((NBLK, BLOCK, WIDTH), BF16),
            pltpu.VMEM((NBLK, NB * BLOCK, BLOCK), F32),
            pltpu.VMEM(blocks, BF16),
            pltpu.VMEM(blocks, BF16),
            pltpu.VMEM((NBLK + 1, BLOCK, HDIM), F32),
            pltpu.VMEM((NBLK + 1, BLOCK, HDIM), F32),
            pltpu.VMEM(blocks, F32),
            pltpu.VMEM(blocks, F32),
            pltpu.VMEM(blocks, BF16),
            pltpu.VMEM(blocks, BF16),
            pltpu.VMEM((BLOCK, WIDTH), BF16),
            pltpu.VMEM((BLOCK, WIDTH), F32),
            pltpu.VMEM((BLOCK, WIDTH), BF16),
            pltpu.VMEM((HALF, WIDTH), BF16),
            pltpu.VMEM((HALF, WIDTH), F32),
            pltpu.VMEM((HALF, WIDTH), BF16),
            pltpu.VMEM((QUART, WIDTH), BF16),
            pltpu.VMEM((QUART, WIDTH), BF16),
            pltpu.VMEM((max(rows_y - 1, 1), wrow, wcol), BF16),
            pltpu.VMEM((wrow, wcol), BF16),
            pltpu.SMEM((1, NB, NBLK), jnp.int32),
            pltpu.SemaphoreType.DMA((3,)),
            pltpu.SemaphoreType.DMA((3,)),
            pltpu.SemaphoreType.DMA((16, 2)),
            pltpu.SemaphoreType.DMA((3,)),
            pltpu.SemaphoreType.DMA((6,)),
            pltpu.SemaphoreType.DMA((9,)),
            pltpu.SemaphoreType.DMA((6,)),
        ],
        compiler_params=pltpu.CompilerParams(
            collective_id=0, has_side_effects=True, vmem_limit_bytes=60 * 1024 * 1024
        ),
        cost_estimate=pl.CostEstimate(flops=4_000_000_000, bytes_accessed=8_000_000, transcendentals=1_000_000),
    )(queries, keys_in, values, out_grad, out_weight, jnp.transpose(block_lists, (0, 2, 1)), voxel_count)

    def hand_over(*refs):
        ins, outs, held, sems = refs[:4], refs[4:8], refs[8], refs[9]
        reads = [pltpu.make_async_copy(src, held.at[i], sems.at[0, i]) for i, src in enumerate(ins)]
        writes = [pltpu.make_async_copy(held.at[i], dst, sems.at[1, i]) for i, dst in enumerate(outs)]
        for copy in reads:
            copy.start()
        for read, write in zip(reads, writes):
            read.wait()
            write.start()
        for copy in writes:
            copy.wait()

    return pl.pallas_call(
        hand_over,
        out_shape=(rows, rows, rows, rows),
        in_specs=[hbm] * 4,
        out_specs=(hbm,) * 4,
        scratch_shapes=[pltpu.VMEM((4, BLOCK, WIDTH), BF16), pltpu.SemaphoreType.DMA((2, 4))],
        compiler_params=pltpu.CompilerParams(vmem_limit_bytes=60 * 1024 * 1024),
    )(*grads)


def solution(mesh):
    return jax.shard_map(
        body,
        mesh=mesh,
        in_specs=(
            P(("dp", "shard"), None),
            P(("dp", "shard"), None),
            P(("dp", "shard"), None),
            P(("dp", "shard"), None),
            P("shard", None),
            P("dp", None, None),
            P("dp"),
        ),
        out_specs=(
            P(("dp", "shard"), None),
            P(("dp", "shard"), None),
            P(("dp", "shard"), None),
            P("shard", None),
        ),
        check_vma=False,
    )
```

```python
import math

import jax
import jax.numpy as jnp
from jax import lax
from jax.experimental import pallas as pl
from jax.experimental.pallas import tpu as pltpu
from jax.sharding import PartitionSpec as P

HDIM = 128
BLOCK = 128
NB = 4
NBLK = 16
WIDTH = 2048
HALF = BLOCK // 2
QUART = BLOCK // 4
SCALE = 1.0 / math.sqrt(HDIM)
LOG2E = math.log2(math.e)
F32 = jnp.float32
BF16 = jnp.bfloat16
MESH = pl.DeviceIdType.MESH

NT = (((1,), (1,)), ((), ()))
NN = (((1,), (0,)), ((), ()))


def dot(a, b, dims):
    return lax.dot_general(a, b, dims, preferred_element_type=F32)


def order(i):
    return i + i // 2 - 2 * (i // 3)


def kernel(
    parts,
    q_in, k_in, v_in, g_in, w_in, lists_in, count,
    dq_out, dk_out, dv_out, dw_out,
    da, qx, kx, vx, qh, kh, vh, kt, vt, gall, probs, heads, dqb, kpart, vpart, kacc, vacc, dkb, dvb,
    w_ref, wacc, wbf, wcore, whalf, whbf, wquart, wqbf, wrecv, wres,
    lists, x_recv, qkv_recv, g_recv, out_recv, w_recv, send_sem, local_sem,
):
    me = lax.axis_index("shard")
    scene = lax.axis_index("dp")
    row_parts, col_parts = parts
    rows_y = row_parts * col_parts
    scenes = 4 * rows_y
    wrow, wcol = QUART // row_parts, WIDTH // col_parts
    core, low, y = scene % 2, (scene // 2) % 2, scene // 4
    x, z = me // 4, me % 4
    x_up, x_down = ((x + 1) % 4) * 4 + z, ((x + 3) % 4) * 4 + z
    z_up, z_down = x * 4 + (z + 1) % 4, x * 4 + (z + 3) % 4
    live = count[0]

    def columns(index):
        return pl.ds(pl.multiple_of(index * HDIM, HDIM), HDIM)

    def heads_of(index):
        return pl.ds(pl.multiple_of(index * 4 * HDIM, 4 * HDIM), 4 * HDIM)

    own = [
        pltpu.make_async_copy(g_in, gall.at[me], local_sem.at[0]),
        pltpu.make_async_copy(q_in.at[:, heads_of(x)], qx.at[x], local_sem.at[1]),
        pltpu.make_async_copy(k_in.at[:, heads_of(x)], kx.at[x], local_sem.at[2]),
        pltpu.make_async_copy(v_in.at[:, heads_of(x)], vx.at[x], local_sem.at[3]),
        pltpu.make_async_copy(w_in, w_ref, local_sem.at[4]),
        pltpu.make_async_copy(lists_in, lists, local_sem.at[5]),
    ]
    for copy in own:
        copy.start()

    barrier = pltpu.get_barrier_semaphore()

    @pl.loop(1, NBLK)
    def _(o):
        pl.semaphore_signal(barrier, inc=1, device_id={"shard": (me + o) % NBLK}, device_id_type=MESH)

    @pl.loop(1, rows_y)
    def _(o):
        pl.semaphore_signal(
            barrier, inc=1, device_id={"dp": ((y + o) % rows_y) * 4 + scene % 4}, device_id_type=MESH
        )

    other_core = scene + 1 - 2 * core
    other_low = scene + 2 - 4 * low
    for peer in (other_core, other_low):
        pl.semaphore_signal(barrier, inc=1, device_id={"dp": peer}, device_id_type=MESH)
    pl.semaphore_wait(barrier, NBLK - 1 + rows_y - 1 + 2)

    def push(src, dst, send, recv, shard):
        pltpu.make_async_remote_copy(
            src_ref=src, dst_ref=dst, send_sem=send, recv_sem=recv,
            device_id={"shard": shard}, device_id_type=MESH,
        ).start()

    def push_dp(src, dst, send, recv, peer):
        pltpu.make_async_remote_copy(
            src_ref=src, dst_ref=dst, send_sem=send, recv_sem=recv,
            device_id={"dp": peer}, device_id_type=MESH,
        ).start()

    def await_bytes(ref, sem):
        pltpu.make_async_copy(ref, ref, sem).wait()

    def block_at(dx, dz):
        return ((x + dx) % 4) * 4 + (z + dz) % 4

    def g_ref(dx, dz, half):
        return gall.at[block_at(dx, dz), pl.ds(half * HALF, HALF)]

    def g_push(dx, dz, half, target, rdx, rdz):
        src = g_in.at[pl.ds(half * HALF, HALF)] if (dx, dz) == (0, 0) else g_ref(dx, dz, half)
        push(src, g_ref(dx, dz, half), send_sem.at[0], g_recv.at[rdx * 4 + rdz, half], target)

    def g_wait(dx, dz, half):
        await_bytes(g_ref(dx, dz, half), g_recv.at[dx * 4 + dz, half])

    def along_x(dz, half):
        g_push(0, dz, half, x_up, 3, dz)
        g_push(0, dz, half, x_down, 1, dz)

    def pass_up(dz):
        g_wait(3, dz, 0)
        g_push(3, dz, 0, x_up, 2, dz)

    def pass_down(dz):
        g_wait(1, dz, 1)
        g_push(1, dz, 1, x_down, 2, dz)

    arrays = ((q_in, qx, qh), (k_in, kx, kh), (v_in, vx, vh))
    for i, (src, mid, dst) in enumerate(arrays):
        for o in (1, 3, 2):
            to_x = (x + o) % 4
            push(src.at[:, heads_of(to_x)], mid.at[x], send_sem.at[8], x_recv.at[i], to_x * 4 + z)

    g_push(0, 0, 0, z_up, 0, 3)
    g_push(0, 0, 1, z_down, 0, 1)
    g_push(0, 0, 0, x_up, 3, 0)
    g_push(0, 0, 1, x_down, 1, 0)
    g_push(0, 0, 1, x_up, 3, 0)
    g_push(0, 0, 0, x_down, 1, 0)
    kacc[...] = jnp.zeros_like(kacc)
    vacc[...] = jnp.zeros_like(vacc)
    wacc[...] = jnp.zeros_like(wacc)
    kpart[NBLK] = jnp.zeros_like(kpart[NBLK])
    vpart[NBLK] = jnp.zeros_like(vpart[NBLK])
    for copy in own:
        copy.wait()

    def along_z(i):
        src, mid, dst = arrays[i]
        await_bytes(mid.at[pl.ds(0, 3)], x_recv.at[i])
        for o in (1, 3, 2):
            to_z = (z + o) % 4
            push(mid.at[:, :, columns(to_z)], dst.at[:, z], send_sem.at[8], qkv_recv.at[i], x * 4 + to_z)
        pltpu.make_async_copy(mid.at[:, :, columns(z)], dst.at[:, z], local_sem.at[i]).start()

    g_wait(0, 3, 0)
    g_push(0, 3, 0, z_up, 0, 2)
    along_x(3, 0)
    g_wait(0, 1, 1)
    g_push(0, 1, 1, z_down, 0, 2)
    along_x(1, 1)
    for i in range(3):
        along_z(i)
    pass_up(0)
    pass_down(0)
    for half in range(2):
        g_wait(0, 2, half)
        along_x(2, half)
    pass_up(3)
    pass_down(1)
    pass_up(2)
    pass_down(2)

    g_push(0, 0, 1, z_up, 0, 3)
    g_push(0, 0, 0, z_down, 0, 1)
    lane = lax.broadcasted_iota(jnp.int32, (BLOCK, BLOCK), 1)
    sublane = lax.broadcasted_iota(jnp.int32, (BLOCK, BLOCK), 0)

    def grad_attn(b):
        dead_query = (b * BLOCK + lane) >= live
        return jnp.where(dead_query, 0.0, dot(w_ref[...], gall[b], NT)).astype(BF16)

    g_wait(3, 0, 1)
    g_wait(1, 0, 0)
    g_wait(2, 0, 0)
    g_wait(2, 0, 1)

    @pl.loop(0, 4)
    def _(i):
        b = block_at(i, 0)
        da[b] = grad_attn(b)

    da[block_at(0, 2)] = grad_attn(block_at(0, 2))

    for i, (src, mid, dst) in enumerate(arrays):
        await_bytes(dst.at[pl.ds(0, 3)], qkv_recv.at[i])
        pltpu.make_async_copy(mid.at[:, :, columns(z)], dst.at[:, z], local_sem.at[i]).wait()

    @pl.loop(0, NBLK)
    def _(b):
        kt[b] = kh[b // 4, b % 4].T
        vt[b] = vh[b // 4, b % 4].T

    def forward(b):
        ids = [lists[0, j, b] for j in range(NB)]
        keys = jnp.concatenate([kh[c // 4, c % 4] for c in ids], axis=0)
        scores = dot(keys, qh[b // 4, b % 4], NT) * (SCALE * LOG2E)
        query_pos = b * BLOCK + lane
        dead_query = query_pos >= live
        allowed = jnp.concatenate([((c * BLOCK + sublane) < live) | dead_query for c in ids], axis=0)
        scores = jnp.where(allowed, scores, -jnp.inf)
        peak = jnp.max(scores, axis=0, keepdims=True)
        weights = jnp.exp2(scores - peak)
        prob = weights * (1.0 / jnp.sum(weights, axis=0, keepdims=True))
        probs[b] = prob
        values_t = jnp.concatenate([vt[c] for c in ids], axis=1)
        head_t = dot(values_t, prob.astype(BF16), NN)
        heads[b] = jnp.where(dead_query, 0.0, head_t).astype(BF16)

    pl.loop(0, NBLK // 2, unroll=4)(forward)
    g_wait(0, 3, 1)
    along_x(3, 1)
    g_wait(0, 1, 0)
    along_x(1, 0)
    pl.loop(NBLK // 2, NBLK, unroll=4)(forward)

    def backward(slot, b, early=False):
        ids = [lists[0, j, b] for j in range(NB)]
        da_t = da[b] if early else grad_attn(b)
        prob = probs[b]
        grad_prob = dot(jnp.concatenate([vh[c // 4, c % 4] for c in ids], axis=0), da_t, NN)
        delta = jnp.sum(prob * grad_prob, axis=0, keepdims=True)
        dscore = (prob * (grad_prob - delta) * SCALE).astype(BF16)
        keys_t = jnp.concatenate([kt[c] for c in ids], axis=1)
        dqb[b] = dot(keys_t, dscore, NN).T.astype(BF16)
        at = pl.ds(slot * NB, NB)
        kpart[at] = dot(dscore, qh[b // 4, b % 4], NN).reshape(NB, BLOCK, HDIM)
        vpart[at] = dot(prob.astype(BF16), da_t, NT).reshape(NB, BLOCK, HDIM)

    def add_parts(blocks):
        ids = [[lists[0, j, b] for j in range(NB)] for b in blocks]

        @pl.loop(0, NBLK)
        def _(c):
            key, value = kacc[c], vacc[c]
            for slot in range(NB):
                place = NBLK
                for j in range(NB):
                    place = jnp.where(ids[slot][j] == c, slot * NB + j, place)
                key = key + kpart[place]
                value = value + vpart[place]
            kacc[c] = key
            vacc[c] = value

    tile = 256

    def add_weight(blocks):
        head = jnp.concatenate([heads[b] for b in blocks], axis=1)

        @pl.loop(0, WIDTH // tile)
        def _(t):
            at = pl.ds(pl.multiple_of(t * tile, tile), tile)
            grad = jnp.concatenate([gall[b, :, at] for b in blocks], axis=0)
            wacc[:, at] += dot(head, grad, NN)

    def send_dq(b):
        push(dqb.at[b], dq_out.at[:, columns(me)], send_sem.at[1], out_recv.at[0], b)

    for dz in (2,):
        g_wait(3, dz, 1)
        g_wait(1, dz, 0)
        g_wait(2, dz, 0)
        g_wait(2, dz, 1)

    for dz in (0, 2):
        for i in range(0, 4, 2):
            for j in range(2):
                backward(i + j, block_at(i + j, dz), early=dz == 0 or i + j == 0)
            for j in range(2):
                if dz + i + j > 0:
                    send_dq(block_at(i + j, dz))

        blocks = [block_at(dx, dz) for dx in range(4)]
        add_parts(blocks)
        add_weight(blocks)

    pass_down(3)
    pass_up(1)

    for dz in (3, 1):
        g_wait(3, dz, 1)
        g_wait(1, dz, 0)

    @pl.loop(0, 2)
    def _(i):
        pair = [block_at(3 * i, dz) for dz in (3, 1)]
        for j in range(2):
            backward(2 * i + j, pair[j])
        for b in pair:
            send_dq(b)

    blocks = [block_at(dx, dz) for dx in (0, 3) for dz in (3, 1)]
    add_parts(blocks)
    near, far = [[block_at(dx, dz) for dz in (3, 1)] for dx in (1, 2)]

    for i in range(2):
        backward(i, near[i])
    for b in near:
        send_dq(b)

    add_weight(blocks + near)
    for dz in (3, 1):
        g_wait(2, dz, 0)
        g_wait(2, dz, 1)
    add_weight(far)
    wbf[...] = wacc[...].astype(BF16)

    def rows_at(index, size):
        return pl.ds(pl.multiple_of(index * size, size), size)

    push_dp(wbf.at[rows_at(1 - core, HALF)], wcore, send_sem.at[2], w_recv.at[0], other_core)

    for i in range(2):
        backward(2 + i, far[i])
    for b in far:
        send_dq(b)

    await_bytes(wcore, w_recv.at[0])
    whalf[...] = wacc[rows_at(core, HALF)] + wcore[...].astype(F32)
    whbf[...] = whalf[...].astype(BF16)
    push_dp(whbf.at[rows_at(1 - low, QUART)], wquart, send_sem.at[3], w_recv.at[1], other_low)

    add_parts(near + far)
    dvb[...] = vacc[...].astype(BF16)

    @pl.loop(1, NBLK)
    def _(o):
        peer = (me + o) % NBLK
        push(dvb.at[peer], dv_out.at[:, columns(me)], send_sem.at[1], out_recv.at[2], peer)

    dkb[...] = kacc[...].astype(BF16)

    @pl.loop(1, NBLK)
    def _(o):
        peer = (me + o) % NBLK
        push(dkb.at[peer], dk_out.at[:, columns(me)], send_sem.at[1], out_recv.at[1], peer)

    back = [
        pltpu.make_async_copy(src.at[me], dst.at[:, columns(me)], local_sem.at[i])
        for i, (src, dst) in enumerate(((dqb, dq_out), (dkb, dk_out), (dvb, dv_out)))
    ]
    for copy in back:
        copy.start()

    await_bytes(wquart, w_recv.at[1])
    mine = whalf[rows_at(low, QUART)] + wquart[...].astype(F32)
    whalf[pl.ds(0, QUART)] = mine
    wqbf[...] = mine.astype(BF16)

    def piece(index, first=0):
        return (
            pl.ds(pl.multiple_of(first + (index // col_parts) * wrow, wrow), wrow),
            pl.ds(pl.multiple_of((index % col_parts) * wcol, wcol), wcol),
        )

    @pl.loop(1, rows_y)
    def _(o):
        peer = (y + o) % rows_y
        push_dp(wqbf.at[piece(peer)], wrecv.at[o - 1], send_sem.at[4], w_recv.at[2], peer * 4 + scene % 4)

    total = whalf[piece(y)]
    if rows_y > 1:
        await_bytes(wrecv, w_recv.at[2])
        for i in range(rows_y - 1):
            total = total + wrecv[i].astype(F32)
    wres[...] = (total * (1.0 / scenes)).astype(BF16)
    place = dw_out.at[piece(y, core * HALF + low * QUART)]

    @pl.loop(1, rows_y)
    def _(o):
        peer = (y + o) % rows_y
        push_dp(wres, place, send_sem.at[5], w_recv.at[3], peer * 4 + scene % 4)

    keep = pltpu.make_async_copy(wres, place, local_sem.at[3])
    keep.start()
    keep.wait()
    if rows_y > 1:
        await_bytes(wrecv, w_recv.at[3])
    quart = dw_out.at[rows_at(core * 2 + low, QUART)]
    push_dp(quart, quart, send_sem.at[6], w_recv.at[4], other_low)
    await_bytes(wquart, w_recv.at[4])
    half = dw_out.at[rows_at(core, HALF)]
    push_dp(half, half, send_sem.at[7], w_recv.at[5], other_core)

    for copy in back:
        copy.wait()
    for i, out in enumerate((dq_out, dk_out, dv_out)):
        await_bytes(out.at[:, pl.ds(0, WIDTH - HDIM)], out_recv.at[i])
    await_bytes(wcore, w_recv.at[5])
    await_bytes(gall.at[pl.ds(0, NBLK - 1)], send_sem.at[0])
    for dst in (dqb, dkb, dvb):
        await_bytes(dst.at[pl.ds(0, NBLK - 1)], send_sem.at[1])
    for mid in (qx, kx, vx, qx, kx, vx):
        await_bytes(mid.at[pl.ds(0, 3)], send_sem.at[8])
    await_bytes(wcore, send_sem.at[2])
    await_bytes(wquart, send_sem.at[3])
    if rows_y > 1:
        await_bytes(wrecv, send_sem.at[4])
        await_bytes(wrecv, send_sem.at[5])
    await_bytes(wquart, send_sem.at[6])
    await_bytes(wcore, send_sem.at[7])


def body(queries, keys_in, values, out_grad, out_weight, block_lists, voxel_count):
    scenes = lax.axis_size("dp")
    rows_y = scenes // 4
    row_parts = min(2, rows_y)
    col_parts = rows_y // row_parts
    wrow, wcol = QUART // row_parts, WIDTH // col_parts
    blocks = (NBLK, BLOCK, HDIM)
    hbm = pl.BlockSpec(memory_space=pl.ANY)
    smem = pl.BlockSpec(memory_space=pltpu.SMEM)
    rows = jax.ShapeDtypeStruct((BLOCK, WIDTH), BF16)

    def run(*refs):
        kernel((row_parts, col_parts), *refs)

    grads = pl.pallas_call(
        run,
        out_shape=(rows, rows, rows, rows),
        in_specs=[hbm, hbm, hbm, hbm, hbm, hbm, smem],
        out_specs=(hbm, hbm, hbm, hbm),
        scratch_shapes=[
            pltpu.VMEM(blocks, BF16),
            pltpu.VMEM((4, BLOCK, 4 * HDIM), BF16),
            pltpu.VMEM((4, BLOCK, 4 * HDIM), BF16),
            pltpu.VMEM((4, BLOCK, 4 * HDIM), BF16),
            pltpu.VMEM((4, 4, BLOCK, HDIM), BF16),
            pltpu.VMEM((4, 4, BLOCK, HDIM), BF16),
            pltpu.VMEM((4, 4, BLOCK, HDIM), BF16),
            pltpu.VMEM(blocks, BF16),
            pltpu.VMEM(blocks, BF16),
            pltpu.VMEM((NBLK, BLOCK, WIDTH), BF16),
            pltpu.VMEM((NBLK, NB * BLOCK, BLOCK), F32),
            pltpu.VMEM(blocks, BF16),
            pltpu.VMEM(blocks, BF16),
            pltpu.VMEM((NBLK + 1, BLOCK, HDIM), F32),
            pltpu.VMEM((NBLK + 1, BLOCK, HDIM), F32),
            pltpu.VMEM(blocks, F32),
            pltpu.VMEM(blocks, F32),
            pltpu.VMEM(blocks, BF16),
            pltpu.VMEM(blocks, BF16),
            pltpu.VMEM((BLOCK, WIDTH), BF16),
            pltpu.VMEM((BLOCK, WIDTH), F32),
            pltpu.VMEM((BLOCK, WIDTH), BF16),
            pltpu.VMEM((HALF, WIDTH), BF16),
            pltpu.VMEM((HALF, WIDTH), F32),
            pltpu.VMEM((HALF, WIDTH), BF16),
            pltpu.VMEM((QUART, WIDTH), BF16),
            pltpu.VMEM((QUART, WIDTH), BF16),
            pltpu.VMEM((max(rows_y - 1, 1), wrow, wcol), BF16),
            pltpu.VMEM((wrow, wcol), BF16),
            pltpu.SMEM((1, NB, NBLK), jnp.int32),
            pltpu.SemaphoreType.DMA((3,)),
            pltpu.SemaphoreType.DMA((3,)),
            pltpu.SemaphoreType.DMA((16, 2)),
            pltpu.SemaphoreType.DMA((3,)),
            pltpu.SemaphoreType.DMA((6,)),
            pltpu.SemaphoreType.DMA((9,)),
            pltpu.SemaphoreType.DMA((6,)),
        ],
        compiler_params=pltpu.CompilerParams(
            collective_id=0, has_side_effects=True, vmem_limit_bytes=60 * 1024 * 1024
        ),
        cost_estimate=pl.CostEstimate(flops=4_000_000_000, bytes_accessed=8_000_000, transcendentals=1_000_000),
    )(queries, keys_in, values, out_grad, out_weight, jnp.transpose(block_lists, (0, 2, 1)), voxel_count)

    def hand_over(*refs):
        ins, outs, held, sems = refs[:4], refs[4:8], refs[8], refs[9]
        reads = [pltpu.make_async_copy(src, held.at[i], sems.at[0, i]) for i, src in enumerate(ins)]
        writes = [pltpu.make_async_copy(held.at[i], dst, sems.at[1, i]) for i, dst in enumerate(outs)]
        for copy in reads:
            copy.start()
        for read, write in zip(reads, writes):
            read.wait()
            write.start()
        for copy in writes:
            copy.wait()

    return pl.pallas_call(
        hand_over,
        out_shape=(rows, rows, rows, rows),
        in_specs=[hbm] * 4,
        out_specs=(hbm,) * 4,
        scratch_shapes=[pltpu.VMEM((4, BLOCK, WIDTH), BF16), pltpu.SemaphoreType.DMA((2, 4))],
        compiler_params=pltpu.CompilerParams(vmem_limit_bytes=60 * 1024 * 1024),
    )(*grads)


def solution(mesh):
    return jax.shard_map(
        body,
        mesh=mesh,
        in_specs=(
            P(("dp", "shard"), None),
            P(("dp", "shard"), None),
            P(("dp", "shard"), None),
            P(("dp", "shard"), None),
            P("shard", None),
            P("dp", None, None),
            P("dp"),
        ),
        out_specs=(
            P(("dp", "shard"), None),
            P(("dp", "shard"), None),
            P(("dp", "shard"), None),
            P("shard", None),
        ),
        check_vma=False,
    )
```
